128 devices in a mesh: shot: 4 (over y_lo, core), dom: 32 (over y_hi, x, z).
Axes of the slice: x: 4, y: 4 (y_hi: 2, y_lo: 2; y = y_hi * 2 + y_lo), z: 4, core: 2. Of those that a mesh axis runs over, the one named last changes fastest.
Arguments:
- wave_prev: float32 [4, 32, 48, 64, 256], P('shot', 'dom'), may hold values from -6 to 6
- wave_now: float32 [4, 32, 48, 64, 256], P('shot', 'dom'), may hold values from -6 to 6
- stiffness: float32 [32, 48, 64, 256], P('dom'), may hold values from 0.04 to 0.12
- buoyancy: float32 [32, 48, 64, 256], P('dom'), may hold values from 0.6 to 1.4
- snapshots: bfloat16 [4, 4, 32, 48, 64, 256], P('shot', None, 'dom'), may hold values from -4 to 4
- traces: float32 [4, 4, 1024], P('shot'), may hold values from -6 to 6
- aperture: int32 [4, 32], P('shot', 'dom'), may hold values from 0 to 1, as said below
- receivers: int32 [4, 1024, 3], P('shot'), may hold values from 0 to 383, as said below
- sources: int32 [4, 3], P('shot'), may hold values from 0 to 383, as said below
Outputs:
- gradient: float32 [32, 48, 64, 256], P('dom')
- wave_last: float32 [4, 32, 48, 64, 256], P('shot', 'dom')
The draws below stay inside these ranges and needn't reach their ends.
Inputs may be any that keep to these rules, and one draw needn't show every extreme that they name: Each shot's aperture is the tiles whose x position lies in 5 consecutive positions and whose y position lies in 3 consecutive positions. Receiver x indices lie in 0 to 383, y in 0 to 255, z in 0 to 7; receivers may share cells. `sources`: each source lies in the grid, inside its shot's aperture, at a depth under 8.
All inputs are finite; a program needn't handle non-finite values.
Results may differ from the reference program's by a relative error of at most 0.0003.
Values sent between devices are 32-bit elements; how exact they have to be, the bound alone decides.
No kernel may reach another device: no remote copies, remote signals or barrier semaphores. Data moves between devices by JAX's collectives and lax.ppermute only.
A program may use at most 320 MiB of HBM per device.

```python
import math
import jax
import jax.numpy as jnp
from jax import lax

CX = 48
CY = 64
CZ = 256
STEPS = 4
RECS = 1024
MUTE = 6
SHOTS = 4
TILES = 32
NX = 384
NY = 256


def window_starts(key):
    key_x, key_y = jax.random.split(jax.random.fold_in(key, 101))
    tiles_x = NX // CX
    width_x = tiles_x // 2 + 1
    start_x = jax.random.randint(key_x, (SHOTS,), 0, tiles_x - width_x + 1)
    start_y = jax.random.randint(key_y, (SHOTS,), 0, 2)
    start_x = start_x.at[SHOTS - 1].set(tiles_x - width_x)
    start_y = start_y.at[SHOTS - 1].set(1)
    return (start_x, start_y, width_x)


def draw_aperture(key, part):
    start_x, start_y, width_x = window_starts(key)
    tile = jnp.arange(TILES, dtype=jnp.int32)
    pos_x = (tile // 4)[None, :]
    pos_y = (tile % 4)[None, :]
    inside_x = (pos_x >= start_x[:, None]) & (pos_x < start_x[:, None] + width_x)
    inside_y = (pos_y >= start_y[:, None]) & (pos_y < start_y[:, None] + 3)
    return jnp.where(inside_x & inside_y, 1, 0).astype(jnp.int32)


def draw_sources(key, part):
    start_x, start_y, width_x = window_starts(key)
    key = jax.random.fold_in(key, 2)
    key_x, key_y, key_z = jax.random.split(key, 3)
    offset_x = jax.random.randint(key_x, (SHOTS,), 0, width_x * CX)
    offset_y = jax.random.randint(key_y, (SHOTS,), 0, 3 * CY)
    depth = jax.random.randint(key_z, (SHOTS,), 0, min(8, CZ))
    offset_x = offset_x.at[SHOTS - 1].set(width_x * CX - 1)
    offset_y = offset_y.at[SHOTS - 1].set(3 * CY - 1)
    depth = depth.at[0].set(0)
    return jnp.stack([start_x * CX + offset_x, start_y * CY + offset_y, depth], axis=1).astype(jnp.int32)


def draw_receivers(key, part):
    key = jax.random.fold_in(key, 3)
    key_x, key_y, key_z = jax.random.split(key, 3)
    pos_x = jax.random.randint(key_x, (SHOTS, RECS), 0, NX)
    pos_y = jax.random.randint(key_y, (SHOTS, RECS), 0, NY)
    depth = jax.random.randint(key_z, (SHOTS, RECS), 0, min(8, CZ))
    pos_x = pos_x.at[:, 0].set(NX - 1).at[:, 1].set(0)
    pos_y = pos_y.at[:, 0].set(NY - 1).at[:, 1].set(0)
    depth = depth.at[:, 0].set(0).at[:, 1].set(0)
    return jnp.stack([pos_x, pos_y, depth], axis=2).astype(jnp.int32)


def levels(rng, dims, cuts, smallest, largest):
    loudness = 1.0
    for axis_at, blocks in cuts:
        draws = jax.random.uniform(jax.random.fold_in(jax.random.fold_in(rng, 6), axis_at), (blocks,), jnp.float32, smallest / len(cuts), largest / len(cuts))
        loudness = loudness * jnp.repeat(jnp.exp(draws), dims[axis_at] // blocks).reshape((-1,) + (1,) * (len(dims) - 1 - axis_at))
    return loudness


def scatter_about(key, dims, deviation, bound, shards=(), held_as=jnp.bfloat16):
    result = deviation * jax.random.normal(key, dims, jnp.float32)
    if shards:
        result = result * levels(key, dims, shards, -0.22, 0.18)
    return jnp.clip(result, -bound, bound).astype(held_as)


def setup_inputs(seed: int = 0) -> dict:
    key_of = jax.random.split(jax.random.key(seed), 10)
    return {
        "wave_prev": scatter_about(key_of[0], (SHOTS, TILES, CX, CY, CZ), 1.0, 6.0, ((0, 4), (1, 32)), jnp.float32),
        "wave_now": scatter_about(key_of[1], (SHOTS, TILES, CX, CY, CZ), 1.0, 6.0, ((0, 4), (1, 32)), jnp.float32),
        "stiffness": jnp.clip(jnp.exp(math.log(0.12) - 1.0986123 * jax.random.uniform(key_of[2], (TILES, CX, CY, CZ), jnp.float32) ** levels(key_of[2], (TILES, CX, CY, CZ), ((0, 32),), -0.2, 0.2)), 0.04, 0.12),
        "buoyancy": jnp.clip(0.6 + 0.79999995 * jax.random.uniform(key_of[3], (TILES, CX, CY, CZ), jnp.float32) ** levels(key_of[3], (TILES, CX, CY, CZ), ((0, 32),), -0.2, 0.2), 0.6, 1.4),
        "snapshots": scatter_about(key_of[4], (SHOTS, STEPS, TILES, CX, CY, CZ), 0.5, 4.0, ((0, 4), (2, 32))),
        "traces": scatter_about(key_of[5], (SHOTS, STEPS, RECS), 1.0, 6.0, ((0, 4),), jnp.float32),
        "aperture": draw_aperture(jax.random.fold_in(key_of[9], 71), 0),
        "receivers": draw_receivers(jax.random.fold_in(key_of[9], 71), 0),
        "sources": draw_sources(jax.random.fold_in(key_of[9], 71), 0),
    }


second_coef = (-205.0 / 72.0, 8.0 / 5.0, -1.0 / 5.0, 8.0 / 315.0, -1.0 / 560.0)
first_coef = (4.0 / 5.0, -1.0 / 5.0, 4.0 / 105.0, -1.0 / 280.0)


def second_part(extended, axis, length):
    total = jnp.zeros_like(lax.slice_in_dim(extended, 4, 4 + length, axis=axis))
    for step in range(1, 5):
        upper = lax.slice_in_dim(extended, 4 + step, 4 + step + length, axis=axis)
        lower = lax.slice_in_dim(extended, 4 - step, 4 - step + length, axis=axis)
        total = total + second_coef[step] * (upper + lower)
    return total


def first_part(extended, axis, length):
    total = jnp.zeros_like(lax.slice_in_dim(extended, 4, 4 + length, axis=axis))
    for step in range(1, 5):
        upper = lax.slice_in_dim(extended, 4 + step, 4 + step + length, axis=axis)
        lower = lax.slice_in_dim(extended, 4 - step, 4 - step + length, axis=axis)
        total = total + first_coef[step - 1] * (upper - lower)
    return total


def operator(field, x_ext, y_ext, z_ext, buoy, slopes):
    lap = 3.0 * second_coef[0] * field
    lap = lap + second_part(x_ext, 0, field.shape[0]) + second_part(y_ext, 1, field.shape[1]) + second_part(z_ext, 2, field.shape[2])
    flux = slopes[0] * first_part(x_ext, 0, field.shape[0]) + slopes[1] * first_part(y_ext, 1, field.shape[1]) + slopes[2] * first_part(z_ext, 2, field.shape[2])
    return buoy * lap + flux


def padded(field):
    x_ext = jnp.pad(field, ((4, 4), (0, 0), (0, 0)))
    y_ext = jnp.pad(field, ((0, 0), (4, 4), (0, 0)))
    z_ext = jnp.pad(field, ((0, 0), (0, 0), (4, 4)))
    return x_ext, y_ext, z_ext


def to_grid(tiles):
    tiles_x = tiles.shape[0] // 4
    return tiles.reshape(tiles_x, 4, CX, CY, CZ).transpose(0, 2, 1, 3, 4).reshape(tiles_x * CX, 4 * CY, CZ)


def to_tiles(grid):
    tiles_x = grid.shape[0] // CX
    return grid.reshape(tiles_x, CX, 4, CY, CZ).transpose(0, 2, 1, 3, 4).reshape(tiles_x * 4, CX, CY, CZ)


def reference(wave_prev, wave_now, stiffness, buoyancy, snapshots, traces, aperture, receivers, sources):
    stiff = to_grid(stiffness)
    buoy = to_grid(buoyancy)
    bx_ext, by_ext, bz_ext = padded(buoy)
    slopes = (first_part(bx_ext, 0, NX), first_part(by_ext, 1, NY), first_part(bz_ext, 2, CZ))
    grid_x = jnp.arange(NX, dtype=jnp.int32)[:, None, None]
    grid_y = jnp.arange(NY, dtype=jnp.int32)[None, :, None]
    grid_z = jnp.arange(CZ, dtype=jnp.int32)[None, None, :]
    gradient = jnp.zeros((NX, NY, CZ), jnp.float32)
    waves = []
    for shot in range(SHOTS):
        tile_mask = aperture[shot].reshape(NX // CX, 4).astype(jnp.float32)
        cell_mask = jnp.repeat(jnp.repeat(tile_mask, CX, axis=0), CY, axis=1)[:, :, None]
        previous = to_grid(wave_prev[shot])
        current = to_grid(wave_now[shot])
        image = jnp.zeros((NX, NY, CZ), jnp.float32)
        rec = receivers[shot]
        for step in range(STEPS):
            inject = jnp.zeros((NX, NY, CZ), jnp.float32).at[rec[:, 0], rec[:, 1], rec[:, 2]].add(traces[shot, step])
            x_ext, y_ext, z_ext = padded(current)
            change = operator(current, x_ext, y_ext, z_ext, buoy, slopes)
            following = cell_mask * (2.0 * current - previous + stiff * change + inject)
            image = image + to_grid(snapshots[shot, step]).astype(jnp.float32) * following
            previous, current = current, following
        source = sources[shot]
        distance = (grid_x - source[0]) ** 2 + (grid_y - source[1]) ** 2 + (grid_z - source[2]) ** 2
        mute = jnp.where(distance < MUTE * MUTE, 0.0, 1.0).astype(jnp.float32)
        gradient = gradient + mute * image
        waves.append(to_tiles(current))
    return to_tiles(gradient), jnp.stack(waves)
```

```python
import functools

import jax
import jax.numpy as jnp
import ml_dtypes
import numpy as np
from jax import lax
from jax.experimental import pallas as pl
from jax.experimental.pallas import tpu as pltpu
from jax.sharding import PartitionSpec as P

STEPS = 4
MUTE = 6
G = 8
RADIUS = 4

SECOND = (8064.0, -1008.0, 128.0, -9.0)
SECOND_CENTRE = -14350.0
SECOND_SCALE = 5040.0
FIRST = (672.0, -168.0, 32.0, -3.0)
FIRST_SCALE = 840.0

F32 = jnp.float32
BF16 = jnp.bfloat16


def banded(size, weights, odd):
    matrix = np.zeros((size, size + 2 * RADIUS), np.float32)
    for i in range(size):
        for k, w in enumerate(weights, 1):
            matrix[i, i + RADIUS + k] = w
            matrix[i, i + RADIUS - k] = -w if odd else w
    return matrix


def y_matrices(size):
    both = np.concatenate([banded(size, SECOND, False), banded(size, FIRST, True)])
    own = both[:, RADIUS:-RADIUS]
    result = []
    for parity in range(2):
        halo = np.zeros((2 * size, 16), np.float32)
        halo[:, 4 * parity : 4 * parity + 4] = both[:, :RADIUS]
        halo[:, 8 + 4 * parity : 12 + 4 * parity] = both[:, -RADIUS:]
        result.append(np.concatenate([own, own, halo, halo], axis=1))
    return np.stack(result).astype(ml_dtypes.bfloat16)


def z_matrix(size):
    second = banded(size, SECOND, False)[:, RADIUS:-RADIUS].T
    first = banded(size, FIRST, True)[:, RADIUS:-RADIUS].T
    both = np.concatenate([second, first], axis=1)
    return np.concatenate([both, both], axis=0).astype(ml_dtypes.bfloat16)


def parts(value):
    high = value.astype(BF16)
    low = (value - high.astype(F32)).astype(BF16)
    return high, low


def dot(a, b):
    return jnp.dot(a, b, preferred_element_type=F32)


def x_first(window, g):
    total = None
    for k, w in enumerate(FIRST, 1):
        term = w * (window[g + RADIUS + k] - window[g + RADIUS - k])
        total = term if total is None else total + term
    return total


def x_both(window, g):
    second = first = None
    for k in range(1, RADIUS + 1):
        upper, lower = window[g + RADIUS + k], window[g + RADIUS - k]
        s = SECOND[k - 1] * (upper + lower)
        f = FIRST[k - 1] * (upper - lower)
        second = s if second is None else second + s
        first = f if first is None else first + f
    return second, first


def halo_parts(low_ref, high_ref, pair):
    return parts(jnp.concatenate([low_ref[pair], high_ref[pair]], axis=0))


def pack_strips(field, low_ref, high_ref, offset):
    rows = lax.broadcasted_iota(jnp.int32, (8, field.shape[2]), 0)
    last = field.shape[1] - 8

    def body(i, carry):
        even, odd = field[2 * i, 0:8], field[2 * i + 1, 0:8]
        low_ref[offset + i] = jnp.where(rows < 4, even, pltpu.roll(odd, 4, 0))
        even, odd = field[2 * i, last:], field[2 * i + 1, last:]
        high_ref[offset + i] = jnp.where(rows < 4, pltpu.roll(even, 4, 0), odd)
        return carry

    lax.fori_loop(0, field.shape[0] // 2, body, 0, unroll=4)


def strips_kernel(q, b, xl, xh, yl, yh):
    size = q.shape[0]
    for source, at in ((q, 0), (b, RADIUS)):
        xl[at : at + RADIUS] = source[0:RADIUS]
        xh[at : at + RADIUS] = source[size - RADIUS : size]
    pack_strips(q, yl, yh, 0)
    pack_strips(b, yl, yh, size // 2)


def inject_kernel(places, amounts, openness, out, weights):
    pieces = amounts[...]
    high = pieces.astype(BF16).astype(F32)
    rest = pieces - high
    middle = rest.astype(BF16).astype(F32)
    low = rest - middle
    packed = high + pltpu.roll(middle, 32, 1) + pltpu.roll(low, 64, 1)
    weights[...] = packed.astype(BF16)
    size_x, size_y, lanes = out.shape
    block = 4
    receivers = places.shape[1]
    lane = lax.broadcasted_iota(jnp.int32, (block * size_y, lanes), 1)
    scale = openness[0].astype(F32)

    def body(i, carry):
        cells = lax.broadcasted_iota(jnp.int32, (block * size_y, receivers), 0) + i * (block * size_y)
        hit = jnp.where(cells == places[...], 1.0, 0.0).astype(BF16)
        found = dot(hit, weights[...])
        found = found + pltpu.roll(found, lanes - 32, 1) + pltpu.roll(found, lanes - 64, 1)
        found = jnp.where(lane < 32, found * scale, 0.0)
        for j in range(block):
            out[i * block + j] = found[j * size_y : (j + 1) * size_y]
        return carry

    lax.fori_loop(0, size_x // block, body, 0)


def make_coefficients(base, count, plane, r, yl, yh, ymat, zmat, ys, zs, stiff, buoy, coef, scale):
    size_y = r["size_y"]
    pairs = buoy.shape[0] // 2
    for g in range(count):
        high, low = parts(buoy[base + g])
        if g % 2 == 0:
            hh, hl = halo_parts(yl, yh, pairs + (base + g) // 2)
        ys[g, 0:size_y] = dot(ymat[g % 2, size_y:], jnp.concatenate([high, low, hh, hl], axis=0))
        zs[g, :, 0:256] = dot(jnp.concatenate([high, low], axis=1), zmat[:, 256:])
    for row in range(0, size_y, 16):
        for lane in range(0, 256, 128):
            at = (slice(row, row + 16), slice(lane, lane + 128))
            window = [plane(j, at) for j in range(count + 2 * RADIUS)]
            for g in range(count):
                s = stiff[(base + g,) + at] * scale
                t = s * (1.0 / (FIRST_SCALE * FIRST_SCALE))
                coef[0][(base + g,) + at] = s * (1.0 / SECOND_SCALE) * window[g + RADIUS]
                coef[1][(base + g,) + at] = t * x_first(window, g)
                coef[2][(base + g,) + at] = t * ys[(g,) + at]
                coef[3][(base + g,) + at] = t * zs[(g,) + at]


def advance(base, count, plane, r, step, q, p, out, yl, yh, ymat, zmat, ys, zs, coef, inject, snap, image, scale):
    size_y = r["size_y"]
    for g in range(count):
        high, low = parts(q[base + g])
        if g % 2 == 0:
            hh, hl = halo_parts(yl, yh, (base + g) // 2)
        ys[g] = dot(ymat[g % 2], jnp.concatenate([high, low, hh, hl], axis=0))
        zs[g] = dot(jnp.concatenate([high, low], axis=1), zmat[...])
    for row in range(0, size_y, 16):
        for lane in range(0, 256, 128):
            at = (slice(row, row + 16), slice(lane, lane + 128))
            below = (slice(size_y + row, size_y + row + 16), slice(lane, lane + 128))
            beside = (slice(row, row + 16), slice(256 + lane, 256 + lane + 128))
            window = [plane(j, at) for j in range(count + 2 * RADIUS)]
            for g in range(count):
                here = (base + g,) + at
                centre = window[g + RADIUS]
                second, first = x_both(window, g)
                second = (second + 3.0 * SECOND_CENTRE * centre) + (ys[(g,) + at] + zs[(g,) + at])
                change = coef[0][here] * second + coef[1][here] * first
                change = change + coef[2][here] * ys[(g,) + below] + coef[3][here] * zs[(g,) + beside]
                kept = (centre + centre) - p[here]
                if step < 2:
                    kept = kept * scale
                if lane == 0:
                    added = pltpu.roll(inject[base + g, row : row + 16, :], (128 - 8 * step) % 128, 1)
                    depth = lax.broadcasted_iota(jnp.int32, (16, 128), 1)
                    kept = kept + jnp.where(depth < 8, added, 0.0)
                value = kept + change
                out[here] = value
                shown = snap[here].astype(F32) * value
                image[here] = shown if step == 0 else image[here] + shown


def mute(image, source, corner, ranges):
    size_y = image.shape[1]
    y = lax.broadcasted_iota(jnp.int32, (size_y, 128), 0) + corner[1] - source[1]
    z = lax.broadcasted_iota(jnp.int32, (size_y, 128), 1) - source[2]
    flat = y * y + z * z
    for dx in range(1 - MUTE, MUTE):
        at = source[0] - corner[0] + dx
        inside = functools.reduce(lambda a, b: a | b, [(at >= lo) & (at < hi) for lo, hi in ranges])

        @pl.when(inside)
        def _():
            image[at, :, 0:128] = jnp.where(flat + dx * dx < MUTE * MUTE, 0.0, image[at, :, 0:128])


def inner_kernel(step, *refs):
    names = ["q", "p", "snap", "inject", "yl", "yh", "ymat", "zmat", "openness", "source", "corner"]
    names += ["stiff", "buoy"] if step == 0 else ["c0", "c1", "c2", "c3", "image_in"]
    names += ["out", "image"] + (["c0", "c1", "c2", "c3"] if step == 0 else []) + ["ys", "zs"]
    r = dict(zip(names, refs))
    size_x, size_y, _ = r["q"].shape
    r["size_y"] = size_y
    scale = r["openness"][0].astype(F32)
    coef = [r["c%d" % i] for i in range(4)]

    def body(i, carry):
        base = RADIUS + i * G
        common = (r["yl"], r["yh"], r["ymat"], r["zmat"], r["ys"], r["zs"])
        if step == 0:
            plane = lambda j, at: r["buoy"][(base - RADIUS + j,) + at]
            make_coefficients(base, G, plane, r, *common, r["stiff"], r["buoy"], coef, scale)
        plane = lambda j, at: r["q"][(base - RADIUS + j,) + at]
        advance(base, G, plane, r, step, r["q"], r["p"], r["out"], *common, coef, r["inject"], r["snap"], r["image"], scale)
        return carry

    lax.fori_loop(0, (size_x - 2 * RADIUS) // G, body, 0)
    if step == STEPS - 1:
        mute(r["image"], r["source"], r["corner"], [(RADIUS, size_x - RADIUS)])


def outer_kernel(step, *refs):
    names = ["q", "p", "snap", "inject", "yl", "yh", "ymat", "zmat", "openness", "source", "corner", "xl", "xh"]
    names += (["stiff", "buoy"] if step == 0 else []) + ["c0", "c1", "c2", "c3", "image_in"]
    names += ["out", "image"] + (["c0", "c1", "c2", "c3"] if step == 0 else [])
    names += ["sxl", "sxh", "syl", "syh"] if step < STEPS - 1 else []
    names += ["ys", "zs"]
    r = dict(zip(names, refs))
    size_x, size_y, _ = r["q"].shape
    r["size_y"] = size_y
    scale = r["openness"][0].astype(F32)
    coef = [r["c%d" % i] for i in range(4)]
    for base in (0, size_x - RADIUS):

        def reader(field, offset):
            def plane(j, at):
                where = base - RADIUS + j
                if where < 0:
                    return r["xl"][(offset + where + RADIUS,) + at]
                if where >= size_x:
                    return r["xh"][(offset + where - size_x,) + at]
                return field[(where,) + at]

            return plane

        common = (r["yl"], r["yh"], r["ymat"], r["zmat"], r["ys"], r["zs"])
        if step == 0:
            make_coefficients(
                base, RADIUS, reader(r["buoy"], RADIUS), r, *common, r["stiff"], r["buoy"], coef, scale
            )
        advance(
            base, RADIUS, reader(r["q"], 0), r, step, r["q"], r["p"], r["out"], *common, coef, r["inject"],
            r["snap"], r["image"], scale
        )
    if step == STEPS - 1:
        mute(r["image"], r["source"], r["corner"], [(0, RADIUS), (size_x - RADIUS, size_x)])
    else:
        r["sxl"][...] = r["out"][0:RADIUS]
        r["sxh"][...] = r["out"][size_x - RADIUS :]
        pack_strips(r["out"], r["syl"], r["syh"], 0)


VMEM = pl.BlockSpec(memory_space=pltpu.VMEM)
SMEM = pl.BlockSpec(memory_space=pltpu.SMEM)


def call(kernel, name, args, specs, outs, aliases, scratch, flops):
    results = pl.pallas_call(
        kernel,
        name=name,
        in_specs=specs,
        out_specs=[VMEM] * len(outs),
        out_shape=[pltpu.VMEM(shape, F32) for shape in outs],
        input_output_aliases=aliases,
        scratch_shapes=scratch,
        compiler_params=pltpu.CompilerParams(vmem_limit_bytes=12 << 20),
        cost_estimate=pl.CostEstimate(flops=flops, bytes_accessed=1 << 20, transcendentals=0),
    )(*args)
    return list(results)


def exchange(strips):
    sxl, sxh, syl, syh = strips
    tiles = range(lax.axis_size("dom"))
    along_y = [i for i in tiles if i % 4 < 3]
    along_x = [i for i in tiles if i + 4 in tiles]
    yl = lax.ppermute(syh, "dom", [(i, i + 1) for i in along_y])
    yh = lax.ppermute(syl, "dom", [(i + 1, i) for i in along_y])
    xl = lax.ppermute(sxh, "dom", [(i, i + 4) for i in along_x])
    xh = lax.ppermute(sxl, "dom", [(i + 4, i) for i in along_x])
    return xl, xh, yl, yh


def sum_over_shots(image):
    cores = [(i, i ^ 1) for i in range(4)]
    chips = [(i, i ^ 2) for i in range(4)]
    core = lax.axis_index("shot") % 2
    half = image.shape[0] // 2
    sent = lax.dynamic_slice_in_dim(image, (1 - core) * half, half, 0)
    kept = lax.dynamic_slice_in_dim(image, core * half, half, 0)
    mine = kept + lax.ppermute(sent, "shot", cores)
    mine = mine + lax.ppermute(mine, "shot", chips)
    other = lax.ppermute(mine, "shot", cores)
    low = jnp.where(core == 0, mine, other)
    high = jnp.where(core == 0, other, mine)
    return jnp.concatenate([low, high], axis=0)


def on_device(wave_prev, wave_now, stiffness, buoyancy, snapshots, traces, aperture, receivers, sources):
    index = lax.axis_index("dom")
    stiff, buoy = stiffness[0], buoyancy[0]
    size_x, size_y, size_z = buoy.shape
    grid = buoy.shape
    corner = jnp.stack([index // 4 * size_x, index % 4 * size_y]).astype(jnp.int32)
    openness = jnp.where(aperture[0] > 0, 1, 0).astype(jnp.int32)
    source = sources[0]
    q, p = wave_now[0, 0], wave_prev[0, 0]

    rec = receivers[0]
    local_x, local_y = rec[:, 0] - corner[0], rec[:, 1] - corner[1]
    inside = (local_x >= 0) & (local_x < size_x) & (local_y >= 0) & (local_y < size_y)
    places = jnp.where(inside, local_x * size_y + local_y, -1)[None, :]
    lane = jnp.arange(128, dtype=jnp.int32)
    spread = jnp.repeat(jnp.pad(traces[0].T, ((0, 0), (0, 12))), 8, axis=1)
    amounts = jnp.where((rec[:, 2:3] == lane[None, :] % 8) & (lane[None, :] < 32), spread, 0.0)

    ymat, zmat = jnp.asarray(y_matrices(size_y)), jnp.asarray(z_matrix(size_z))

    strips = call(
        strips_kernel, "strips", (q, buoy), [VMEM, VMEM],
        [(2 * RADIUS, size_y, size_z)] * 2 + [(size_x, 8, size_z)] * 2, {}, [], 1 << 20,
    )
    halos = exchange(strips)
    (inject,) = call(
        inject_kernel, "inject", (places, amounts, openness), [VMEM, VMEM, SMEM],
        [(size_x, size_y, 128)], {}, [pltpu.VMEM(amounts.shape, BF16)], 2 << 30,
    )

    work = [pltpu.VMEM((G, 2 * size_y, size_z), F32), pltpu.VMEM((G, size_y, 2 * size_z), F32)]
    coef = image = None
    for step in range(STEPS):
        xl, xh, yl, yh = halos
        snap = snapshots[0, step, 0]
        shared = [snap, inject, yl, yh, ymat, zmat, openness, source, corner]
        specs = [VMEM] * 8 + [SMEM] * 3
        if step == 0:
            args = [q, p] + shared + [stiff, buoy]
            out, image, *coef = call(
                functools.partial(inner_kernel, step), "inner%d" % step, args,
                specs + [VMEM] * 2, [grid] * 6, {1: 0}, work, 4 << 30,
            )
            args = [q, out] + shared + [xl, xh, stiff, buoy] + coef + [image]
            aliases = {1: 0, 19: 1, 15: 2, 16: 3, 17: 4, 18: 5}
            outs = [grid] * 6
        else:
            args = [q, p] + shared + coef + [image]
            out, image = call(
                functools.partial(inner_kernel, step), "inner%d" % step, args,
                specs + [VMEM] * 5, [grid] * 2, {1: 0, 15: 1}, work, 4 << 30,
            )
            args = [q, out] + shared + [xl, xh] + coef + [image]
            aliases = {1: 0, 17: 1}
            outs = [grid] * 2
        if step < STEPS - 1:
            outs = outs + [(RADIUS, size_y, size_z)] * 2 + [(size_x // 2, 8, size_z)] * 2
        results = call(
            functools.partial(outer_kernel, step), "outer%d" % step, args,
            specs + [VMEM] * (len(args) - 11), outs, aliases, work, 1 << 30,
        )
        q, p = results[0], q
        image = results[1]
        if step == 0:
            coef = results[2:6]
        if step < STEPS - 1:
            halos = exchange(results[-4:])
    return sum_over_shots(image)[None], q[None, None]


def solution(mesh):
    return jax.shard_map(
        on_device,
        mesh=mesh,
        in_specs=(
            P("shot", "dom", None, None, None),
            P("shot", "dom", None, None, None),
            P("dom", None, None, None),
            P("dom", None, None, None),
            P("shot", None, "dom", None, None, None),
            P("shot", None, None),
            P("shot", "dom"),
            P("shot", None, None),
            P("shot", None),
        ),
        out_specs=(P("dom", None, None, None), P("shot", "dom", None, None, None)),
        check_vma=False,
    )
```

```python
import functools

import jax
import jax.numpy as jnp
import ml_dtypes
import numpy as np
from jax import lax
from jax.experimental import pallas as pl
from jax.experimental.pallas import tpu as pltpu
from jax.sharding import PartitionSpec as P

STEPS = 4
MUTE = 6
G = 8
RADIUS = 4

SECOND = (8064.0, -1008.0, 128.0, -9.0)
SECOND_CENTRE = -14350.0
SECOND_SCALE = 5040.0
FIRST = (672.0, -168.0, 32.0, -3.0)
FIRST_SCALE = 840.0

F32 = jnp.float32
BF16 = jnp.bfloat16


def banded(size, weights, odd):
    matrix = np.zeros((size, size + 2 * RADIUS), np.float32)
    for i in range(size):
        for k, w in enumerate(weights, 1):
            matrix[i, i + RADIUS + k] = w
            matrix[i, i + RADIUS - k] = -w if odd else w
    return matrix


def y_matrices(size):
    both = np.concatenate([banded(size, SECOND, False), banded(size, FIRST, True)])
    own = both[:, RADIUS:-RADIUS]
    result = []
    for tile, parity in ((0, 0), (0, 1), (1, 0), (1, 1)):
        below, above = 8 * (1 - tile) + 4 * parity, 8 * tile + 4 * parity
        halo = np.zeros((2 * size, 16), np.float32)
        halo[:, below : below + 4] = both[:, :RADIUS]
        halo[:, above : above + 4] = both[:, -RADIUS:]
        result.append(np.concatenate([own, own, halo, halo], axis=1))
    return np.stack(result).astype(ml_dtypes.bfloat16)


def z_matrix(size):
    second = banded(size, SECOND, False)[:, RADIUS:-RADIUS].T
    first = banded(size, FIRST, True)[:, RADIUS:-RADIUS].T
    both = np.concatenate([second, first], axis=1)
    return np.concatenate([both, both], axis=0).astype(ml_dtypes.bfloat16)


def parts(value):
    high = value.astype(BF16)
    low = (value - high.astype(F32)).astype(BF16)
    return high, low


def dot(a, b):
    return jnp.dot(a, b, preferred_element_type=F32)


def x_first(window, g):
    total = None
    for k, w in enumerate(FIRST, 1):
        term = w * (window[g + RADIUS + k] - window[g + RADIUS - k])
        total = term if total is None else total + term
    return total


def x_both(window, g):
    second = first = None
    for k in range(1, RADIUS + 1):
        upper, lower = window[g + RADIUS + k], window[g + RADIUS - k]
        s = SECOND[k - 1] * (upper + lower)
        f = FIRST[k - 1] * (upper - lower)
        second = s if second is None else second + s
        first = f if first is None else first + f
    return second, first


def halo_parts(first_ref, second_ref, pair):
    return parts(jnp.concatenate([first_ref[pair], second_ref[pair]], axis=0))


def pack_strips(lowest, highest, odd_tile, first_ref, second_ref, offset):
    rows = lax.broadcasted_iota(jnp.int32, lowest.shape[1:], 0)

    def body(i, carry):
        even, odd = lowest[2 * i], lowest[2 * i + 1]
        low = jnp.where(rows < 4, even, pltpu.roll(odd, 4, 0))
        even, odd = highest[2 * i], highest[2 * i + 1]
        high = jnp.where(rows < 4, pltpu.roll(even, 4, 0), odd)
        first_ref[offset + i] = jnp.where(odd_tile, low, high)
        second_ref[offset + i] = jnp.where(odd_tile, high, low)
        return carry

    lax.fori_loop(0, lowest.shape[0] // 2, body, 0, unroll=4)


def strips_kernel(q, b, corner, xa, xb, ya, yb, rows, sems):
    size_x, size_y, _ = q.shape
    top = size_x - RADIUS
    copies = []
    for i, source in enumerate((q, b)):
        at = RADIUS * i
        copies += [
            (source.at[:, 0:8], rows.at[i, 0]),
            (source.at[:, size_y - 8 : size_y], rows.at[i, 1]),
            (source.at[pl.ds(top * corner[3], RADIUS)], xa.at[at : at + RADIUS]),
            (source.at[pl.ds(top * (1 - corner[3]), RADIUS)], xb.at[at : at + RADIUS]),
        ]
    copies = [pltpu.make_async_copy(*pair, sems.at[n]) for n, pair in enumerate(copies)]
    for copy in copies:
        copy.start()
    for i in range(2):
        copies[4 * i].wait()
        copies[4 * i + 1].wait()
        pack_strips(rows.at[i, 0], rows.at[i, 1], corner[4] == 1, ya, yb, i * (size_x // 2))
    for i in range(2):
        copies[4 * i + 2].wait()
        copies[4 * i + 3].wait()


def fetch_kernel(places, amounts, openness, corner, *refs):
    count = (len(refs) - 3) // 2
    sources, targets = refs[:count], refs[count + 1 : 2 * count + 1]
    out, (weights, sems) = refs[count], refs[2 * count + 1 :]
    copies = [pltpu.make_async_copy(a, b, sems.at[n]) for n, (a, b) in enumerate(zip(sources, targets))]
    for copy in copies:
        copy.start()
    size_x, size_y, lanes = out.shape
    receivers = amounts.shape[1]
    sublane = lax.broadcasted_iota(jnp.int32, (8, receivers), 0)
    at_depth = sublane == places[2]
    spread = [jnp.where(at_depth, amounts[t : t + 1], 0.0) for t in range(STEPS)]
    spread = jnp.concatenate(spread, axis=0)
    high = spread.astype(BF16).astype(F32)
    rest = spread - high
    middle = rest.astype(BF16).astype(F32)
    pieces = [high, middle, rest - middle, jnp.zeros_like(high)]
    weights[...] = jnp.concatenate(pieces, axis=0).T.astype(BF16)
    block = 8
    scale = openness[0, 0].astype(F32)
    lane = lax.broadcasted_iota(jnp.int32, (block * size_y, lanes), 1)
    local_x = places[0] - corner[0]
    rows = lax.broadcasted_iota(jnp.int32, (size_y, receivers), 0)
    at_y = jnp.where(rows == places[1] - corner[1], 1.0, 0.0).astype(BF16)

    def body(i, carry):
        hits = []
        for j in range(block):
            at_x = jnp.where(local_x == i * block + j, 1.0, 0.0).astype(BF16)
            hits.append(at_y * at_x)
        found = dot(jnp.concatenate(hits, axis=0), weights[...])
        found = found + pltpu.roll(found, lanes - 32, 1) + pltpu.roll(found, lanes - 64, 1)
        found = jnp.where(lane < 32, found * scale, 0.0)
        for j in range(block):
            out[i * block + j] = found[j * size_y : (j + 1) * size_y]
        return carry

    lax.fori_loop(0, size_x // block, body, 0)
    for copy in copies:
        copy.wait()


def make_coefficients(base, count, plane, r, ya, yb, ymat, zmat, ys, zs, stiff, buoy, coef, scale):
    size_y = r["size_y"]
    pairs = buoy.shape[0] // 2
    for g in range(count):
        high, low = parts(buoy[base + g])
        if g % 2 == 0:
            hh, hl = halo_parts(ya, yb, pairs + (base + g) // 2)
        ys[g, 0:size_y] = dot(ymat[r["variant"] + g % 2, size_y:], jnp.concatenate([high, low, hh, hl], axis=0))
        zs[g, :, 0:256] = dot(jnp.concatenate([high, low], axis=1), zmat[:, 256:])
    for row in range(0, size_y, 16):
        for lane in range(0, 256, 128):
            at = (slice(row, row + 16), slice(lane, lane + 128))
            window = [plane(j, at) for j in range(count + 2 * RADIUS)]
            for g in range(count):
                s = stiff[(base + g,) + at] * scale
                t = s * (1.0 / (FIRST_SCALE * FIRST_SCALE))
                coef[0][(base + g,) + at] = s * (1.0 / SECOND_SCALE) * window[g + RADIUS]
                coef[1][(base + g,) + at] = t * x_first(window, g)
                coef[2][(base + g,) + at] = t * ys[(g,) + at]
                coef[3][(base + g,) + at] = t * zs[(g,) + at]


def advance(base, count, plane, r, step, q, p, out, ya, yb, ymat, zmat, ys, zs, coef, inject, snap, image, scale):
    size_y = r["size_y"]
    for g in range(count):
        high, low = parts(q[base + g])
        if g % 2 == 0:
            hh, hl = halo_parts(ya, yb, (base + g) // 2)
        ys[g] = dot(ymat[r["variant"] + g % 2], jnp.concatenate([high, low, hh, hl], axis=0))
        zs[g] = dot(jnp.concatenate([high, low], axis=1), zmat[...])
    elementwise(base, count, plane, r, step, q, p, out, ys, zs, coef, inject, snap, image, scale)


def elementwise(base, count, plane, r, step, q, p, out, ys, zs, coef, inject, snap, image, scale):
    size_y = r["size_y"]
    for row in range(0, size_y, 16):
        for lane in range(0, 256, 128):
            at = (slice(row, row + 16), slice(lane, lane + 128))
            below = (slice(size_y + row, size_y + row + 16), slice(lane, lane + 128))
            beside = (slice(row, row + 16), slice(256 + lane, 256 + lane + 128))
            window = [plane(j, at) for j in range(count + 2 * RADIUS)]
            for g in range(count):
                here = (base + g,) + at
                centre = window[g + RADIUS]
                second, first = x_both(window, g)
                second = (second + 3.0 * SECOND_CENTRE * centre) + (ys[(g,) + at] + zs[(g,) + at])
                change = coef[0][here] * second + coef[1][here] * first
                change = change + coef[2][here] * ys[(g,) + below] + coef[3][here] * zs[(g,) + beside]
                kept = (centre + centre) - p[here]
                if step < 2:
                    kept = kept * scale
                if lane == 0:
                    added = pltpu.roll(inject[base + g, row : row + 16, :], (128 - 8 * step) % 128, 1)
                    depth = lax.broadcasted_iota(jnp.int32, (16, 128), 1)
                    kept = kept + jnp.where(depth < 8, added, 0.0)
                value = kept + change
                out[here] = value
                shown = snap[here].astype(F32) * value
                image[here] = shown if step == 0 else image[here] + shown


def mute(image, source, corner, ranges):
    size_y = image.shape[1]
    y = lax.broadcasted_iota(jnp.int32, (size_y, 128), 0) + corner[1] - source[0, 1]
    z = lax.broadcasted_iota(jnp.int32, (size_y, 128), 1) - source[0, 2]
    flat = y * y + z * z
    for dx in range(1 - MUTE, MUTE):
        at = source[0, 0] - corner[0] + dx
        inside = functools.reduce(lambda a, b: a | b, [(at >= lo) & (at < hi) for lo, hi in ranges])

        @pl.when(inside)
        def _():
            image[at, :, 0:128] = jnp.where(flat + dx * dx < MUTE * MUTE, 0.0, image[at, :, 0:128])


def split_image(image, sent, kept, core, ranges):
    (lower, _), (upper, _) = ranges

    def body(i, carry):
        sent[i] = image[jnp.where(core == 0, upper, lower) + i]
        kept[i] = image[jnp.where(core == 0, lower, upper) + i]
        return carry

    lax.fori_loop(0, sent.shape[0], body, 0)


def step_kernel(step, ranges, edges, splits, names, *refs):
    r = dict(zip(names, refs))
    q, corner = r["q"], r["corner"]
    size_x, size_y, _ = q.shape
    r["size_y"] = size_y
    r["variant"] = 2 * corner[4]
    scale = r["openness"][0, 0].astype(F32)
    coef = [r["c%d" % i] for i in range(4)]
    common = (r["ya"], r["yb"], r["ymat"], r["zmat"], r["ys"], r["zs"])
    if "snap_next" in r:
        copy = pltpu.make_async_copy(r["snaps"].at[step + 1], r["snap_next"], r["sem"])
        copy.start()

    def reader(field, base, offset):
        def plane(j, at):
            where = base - RADIUS + j
            if isinstance(where, int) and where < 0:
                return r["halo"][(0, offset + where + RADIUS) + at]
            if isinstance(where, int) and where >= size_x:
                return r["halo"][(1, offset + where - size_x) + at]
            return field[(where,) + at]

        return plane

    def group(base, count):
        if step == 0:
            make_coefficients(
                base, count, reader(r["buoy"], base, RADIUS), r, *common, r["stiff"], r["buoy"], coef, scale
            )
        advance(
            base, count, reader(q, base, 0), r, step, q, r["p"], r["out"], *common, coef, r["inject"], r["snap"],
            r["image"], scale
        )

    for low, high in ranges:
        count = G if (high - low) % G == 0 else 4

        def body(i, carry):
            group(low + i * count, count)
            return carry

        lax.fori_loop(0, (high - low) // count, body, 0)
    if edges:
        r["halo"][corner[3]] = r["xa"][...]
        r["halo"][1 - corner[3]] = r["xb"][...]
        group(0, RADIUS)
        group(size_x - RADIUS, RADIUS)
        ranges = ranges + [(0, RADIUS), (size_x - RADIUS, size_x)]
    if step == STEPS - 1:
        mute(r["image"], r["source"], corner, ranges)
        for n, halves in enumerate(splits):
            split_image(r["image"], r["sent%d" % n], r["kept%d" % n], corner[2], halves)
    elif edges:
        top = size_x - RADIUS
        r["sxa"][...] = r["out"][pl.ds(top * corner[3], RADIUS)]
        r["sxb"][...] = r["out"][pl.ds(top * (1 - corner[3]), RADIUS)]
        pack_strips(r["out"].at[:, 0:8], r["out"].at[:, size_y - 8 :], corner[4] == 1, r["sya"], r["syb"], 0)
    if "snap_next" in r:
        copy.wait()


def add_kernel(a, b, out):
    out[...] = a[...] + b[...]


def gather_kernel(ranges, corner, mine, other, *refs):
    out, sems = refs[-2:]
    core = corner[2]
    (lower, _), (upper, _) = ranges
    copies = []
    for k, (source, first, second) in enumerate(((mine, lower, upper), (other, upper, lower))):
        at = jnp.where(core == 0, first, second)
        copies.append(pltpu.make_async_copy(source, out.at[pl.ds(at, source.shape[0])], sems.at[k]))
    for copy in copies:
        copy.start()
    for copy in copies:
        copy.wait()


def store_kernel(source, out, sem):
    copy = pltpu.make_async_copy(source, out, sem)
    copy.start()
    copy.wait()


VMEM = pl.BlockSpec(memory_space=pltpu.VMEM)
SMEM = pl.BlockSpec(memory_space=pltpu.SMEM)
HBM = pl.BlockSpec(memory_space=pltpu.HBM)


def placed(args, specs):
    return [a if s is SMEM else pltpu.with_memory_space_constraint(a, s.memory_space) for a, s in zip(args, specs)]


def call(kernel, name, args, specs, outs, aliases={}, scratch=(), weight=1):
    outs = [pltpu.VMEM(o, F32) if isinstance(o, tuple) else o for o in outs]
    results = pl.pallas_call(
        kernel,
        name=name,
        in_specs=specs,
        out_specs=[pl.BlockSpec(memory_space=o.memory_space) for o in outs],
        out_shape=outs,
        input_output_aliases=aliases,
        scratch_shapes=list(scratch),
        compiler_params=pltpu.CompilerParams(vmem_limit_bytes=8 << 20),
        cost_estimate=pl.CostEstimate(flops=weight, bytes_accessed=1, transcendentals=0),
    )(*placed(args, specs))
    return list(results)


def exchange(strips):
    sxa, sxb, sya, syb = strips

    def swap(strip, stride, odd):
        tiles = range(lax.axis_size("dom"))
        position = lambda i: i % 4 if stride == 1 else i // 4
        last = 3 if stride == 1 else len(tiles) // 4 - 1
        pairs = [(i, i + stride) for i in tiles if position(i) % 2 == odd and position(i) < last]
        return lax.ppermute(strip, "dom", pairs + [(b, a) for a, b in pairs])

    ya, yb = swap(sya, 1, 0), swap(syb, 1, 1)
    xa, xb = swap(sxa, 4, 1), swap(sxb, 4, 0)
    return xa, xb, ya, yb


def sum_over_shots(sent, kept):
    cores = [(i, i ^ 1) for i in range(4)]
    chips = [(i, i ^ 2) for i in range(4)]
    shape = sent.shape
    (mine,) = call(add_kernel, "add_cores", (kept, lax.ppermute(sent, "shot", cores)), [VMEM] * 2, [shape])
    (mine,) = call(add_kernel, "add_chips", (mine, lax.ppermute(mine, "shot", chips)), [VMEM] * 2, [shape])
    return mine, lax.ppermute(mine, "shot", cores)


def on_device(wave_prev, wave_now, stiffness, buoyancy, snapshots, traces, aperture, receivers, sources):
    index = lax.axis_index("dom")
    size_x, size_y, size_z = grid = buoyancy.shape[1:]
    corner = [index // 4 * size_x, index % 4 * size_y, lax.axis_index("shot") % 2, index // 4 % 2, index % 2]
    corner = jnp.stack(corner).astype(jnp.int32)
    places = receivers[0].T[:, None, :]
    ymat, zmat = jnp.asarray(y_matrices(size_y)), jnp.asarray(z_matrix(size_z))
    snaps = snapshots[0, :, 0]

    strips = call(
        strips_kernel, "strips", (wave_now[0, 0], buoyancy[0], corner), [HBM, HBM, SMEM],
        [(2 * RADIUS, size_y, size_z)] * 2 + [(size_x, 8, size_z)] * 2,
        scratch=[pltpu.VMEM((2, 2, size_x, 8, size_z), F32), pltpu.SemaphoreType.DMA((8,))],
    )
    halos = exchange(strips)
    fetched = [wave_now[0, 0], wave_prev[0, 0], buoyancy[0], stiffness[0], ymat, zmat]
    args = [places, traces[0], aperture, corner] + fetched
    inject, q, p, buoy, stiff, ymat, zmat = call(
        fetch_kernel, "fetch", args, [VMEM, VMEM, SMEM, SMEM] + [HBM] * len(fetched),
        [(size_x, size_y, 128)] + [pltpu.VMEM(a.shape, a.dtype) for a in fetched],
        scratch=[pltpu.VMEM((traces.shape[2], 128), BF16), pltpu.SemaphoreType.DMA((len(fetched),))],
    )

    held = dict(inject=inject, ymat=ymat, zmat=zmat, openness=aperture, source=sources, corner=corner, snaps=snaps)
    held.update(buoy=buoy, stiff=stiff, snap=snapshots[0, 0, 0])
    places_of = dict(openness=SMEM, source=SMEM, corner=SMEM, snaps=HBM)

    def run(step, ranges, edges, started, extra, splits=(), weight=1):
        ahead = not edges and step < STEPS - 1
        ins = ["q", "p", "snap", "inject", "ya", "yb", "ymat", "zmat", "openness", "source", "corner"]
        ins += (["xa", "xb"] if edges else []) + (["snaps"] if ahead else [])
        ins += ["stiff", "buoy"] if step == 0 else ["c0", "c1", "c2", "c3"]
        results = ["out", "image"] + (["c0", "c1", "c2", "c3"] if step == 0 else [])
        given = [n for n in results if n in started]
        extra = dict(extra)
        scratch = dict(
            ys=pltpu.VMEM((G, 2 * size_y, size_z), F32), zs=pltpu.VMEM((G, size_y, 2 * size_z), F32)
        )
        if ahead:
            extra["snap_next"] = pltpu.VMEM(grid, snaps.dtype)
            scratch["sem"] = pltpu.SemaphoreType.DMA
        if edges:
            scratch["halo"] = pltpu.VMEM((2,) + held["xa"].shape, F32)
        names = ins + [n + "_in" for n in given] + results + list(extra) + list(scratch)
        outs = call(
            functools.partial(step_kernel, step, ranges, edges, splits, names), "step%d" % step,
            [held[n] for n in ins + given], [places_of.get(n, VMEM) for n in ins + given],
            [grid] * len(results) + list(extra.values()),
            {len(ins) + i: results.index(n) for i, n in enumerate(given)}, scratch.values(), weight,
        )
        held.update(zip(results, outs))
        return outs[len(results) :]

    inner = [(RADIUS, size_x - RADIUS)]
    strip_x, strip_y = (RADIUS, size_y, size_z), (size_x // 2, 8, size_z)
    first = ("out", "image", "c0", "c1", "c2", "c3")
    held.update(q=q, p=p)
    for step in range(STEPS - 1):
        held.update(zip(("xa", "xb", "ya", "yb"), halos))
        (snap_next,) = run(step, inner, False, ("image",) if step else (), {}, weight=4 << 30)
        extra = dict(sxa=strip_x, sxb=strip_x, sya=strip_y, syb=strip_y)
        halos = exchange(run(step, [], True, first if step == 0 else ("out", "image"), extra))
        held.update(q=held["out"], p=held["q"], snap=snap_next)

    held.update(zip(("xa", "xb", "ya", "yb"), halos))
    kernels = [
        ([(16, 32)], False, [((16, 24), (24, 32))]),
        ([(4, 16), (32, 44)], True, [((8, 16), (32, 40)), ((0, 8), (40, 48))]),
    ]
    gradient = None
    for n, (ranges, edges, splits) in enumerate(kernels):
        halves = {}
        for i, (lower, _) in enumerate(splits):
            half = (lower[1] - lower[0], size_y, size_z)
            halves.update({"sent%d" % i: half, "kept%d" % i: half})
        halves = run(STEPS - 1, ranges, edges, ("out", "image") if n else ("image",), halves, splits)
        for i, ranges in enumerate(splits):
            mine, other = sum_over_shots(*halves[2 * i : 2 * i + 2])
            started = [] if gradient is None else [gradient]
            (gradient,) = call(
                functools.partial(gather_kernel, ranges), "gather", [corner, mine, other] + started,
                [SMEM, VMEM, VMEM] + [HBM] * len(started), [pltpu.HBM(grid, F32)], {3: 0} if started else {},
                [pltpu.SemaphoreType.DMA((2,))],
            )
    (last,) = call(store_kernel, "store", [held["out"]], [VMEM], [pltpu.HBM(grid, F32)], {}, [pltpu.SemaphoreType.DMA])
    return gradient[None], last[None, None]


def solution(mesh):
    return jax.shard_map(
        on_device,
        mesh=mesh,
        in_specs=(
            P("shot", "dom", None, None, None),
            P("shot", "dom", None, None, None),
            P("dom", None, None, None),
            P("dom", None, None, None),
            P("shot", None, "dom", None, None, None),
            P("shot", None, None),
            P("shot", "dom"),
            P("shot", None, None),
            P("shot", None),
        ),
        out_specs=(P("dom", None, None, None), P("shot", "dom", None, None, None)),
        check_vma=False,
    )
```

```python
import functools

import jax
import jax.numpy as jnp
import ml_dtypes
import numpy as np
from jax import lax
from jax.experimental import pallas as pl
from jax.experimental.pallas import tpu as pltpu
from jax.sharding import PartitionSpec as P

STEPS = 4
MUTE = 6
G = 8
RADIUS = 4

SECOND = (8064.0, -1008.0, 128.0, -9.0)
SECOND_CENTRE_Y, SECOND_CENTRE_Z = -43008.0, -42.0
SECOND_SCALE = 5040.0
FIRST = (672.0, -168.0, 32.0, -3.0)
FIRST_SCALE = 840.0

F32 = jnp.float32
BF16 = jnp.bfloat16


def banded(size, weights, odd, centre=0.0):
    matrix = np.zeros((size, size + 2 * RADIUS), np.float32)
    for i in range(size):
        matrix[i, i + RADIUS] = centre
        for k, w in enumerate(weights, 1):
            matrix[i, i + RADIUS + k] = w
            matrix[i, i + RADIUS - k] = -w if odd else w
    return matrix


def y_matrices(size):
    both = np.concatenate([banded(size, SECOND, False, SECOND_CENTRE_Y), banded(size, FIRST, True)])
    own = both[:, RADIUS:-RADIUS]
    result = []
    for tile, parity in ((0, 0), (0, 1), (1, 0), (1, 1)):
        below, above = 8 * (1 - tile) + 4 * parity, 8 * tile + 4 * parity
        halo = np.zeros((2 * size, 16), np.float32)
        halo[:, below : below + 4] = both[:, :RADIUS]
        halo[:, above : above + 4] = both[:, -RADIUS:]
        result.append(np.concatenate([own, own, halo, halo], axis=1))
    return np.stack(result).astype(ml_dtypes.bfloat16)


def z_matrix(size):
    second = banded(size, SECOND, False, SECOND_CENTRE_Z)[:, RADIUS:-RADIUS].T
    first = banded(size, FIRST, True)[:, RADIUS:-RADIUS].T
    both = np.concatenate([second, first], axis=1)
    return np.concatenate([both, both], axis=0).astype(ml_dtypes.bfloat16)


def parts(value):
    high = value.astype(BF16)
    low = (value - high.astype(F32)).astype(BF16)
    return high, low


def dot(a, b):
    return jnp.dot(a, b, preferred_element_type=F32)


def x_first(window, g):
    total = None
    for k, w in enumerate(FIRST, 1):
        term = w * (window[g + RADIUS + k] - window[g + RADIUS - k])
        total = term if total is None else total + term
    return total


def x_both(window, g):
    second = first = None
    for k in range(1, RADIUS + 1):
        upper, lower = window[g + RADIUS + k], window[g + RADIUS - k]
        s = SECOND[k - 1] * (upper + lower)
        f = FIRST[k - 1] * (upper - lower)
        second = s if second is None else second + s
        first = f if first is None else first + f
    return second, first


def halo_parts(first_ref, second_ref, pair):
    return parts(jnp.concatenate([first_ref[pair], second_ref[pair]], axis=0))


def pack_strips(lowest, highest, odd_tile, first_ref, second_ref, offset):
    rows = lax.broadcasted_iota(jnp.int32, lowest.shape[1:], 0)

    def body(i, carry):
        even, odd = lowest[2 * i], lowest[2 * i + 1]
        low = jnp.where(rows < 4, even, pltpu.roll(odd, 4, 0))
        even, odd = highest[2 * i], highest[2 * i + 1]
        high = jnp.where(rows < 4, pltpu.roll(even, 4, 0), odd)
        first_ref[offset + i] = jnp.where(odd_tile, low, high)
        second_ref[offset + i] = jnp.where(odd_tile, high, low)
        return carry

    lax.fori_loop(0, lowest.shape[0] // 2, body, 0, unroll=4)


def strips_kernel(q, b, corner, xa, xb, ya, yb, rows, sems):
    size_x, size_y, _ = q.shape
    top = size_x - RADIUS
    copies = []
    for i, source in enumerate((q, b)):
        at = RADIUS * i
        copies += [
            (source.at[:, 0:8], rows.at[i, 0]),
            (source.at[:, size_y - 8 : size_y], rows.at[i, 1]),
            (source.at[pl.ds(top * corner[3], RADIUS)], xa.at[at : at + RADIUS]),
            (source.at[pl.ds(top * (1 - corner[3]), RADIUS)], xb.at[at : at + RADIUS]),
        ]
    copies = [pltpu.make_async_copy(*pair, sems.at[n]) for n, pair in enumerate(copies)]
    for copy in copies:
        copy.start()
    for i in range(2):
        copies[4 * i].wait()
        copies[4 * i + 1].wait()
        pack_strips(rows.at[i, 0], rows.at[i, 1], corner[4] == 1, ya, yb, i * (size_x // 2))
    for i in range(2):
        copies[4 * i + 2].wait()
        copies[4 * i + 3].wait()


def fetch_kernel(places, amounts, openness, corner, *refs):
    count = (len(refs) - 3) // 2
    sources, targets = refs[:count], refs[count + 1 : 2 * count + 1]
    out, (weights, sems) = refs[count], refs[2 * count + 1 :]
    sources = [a if a.shape == b.shape else a.at[0] for a, b in zip(sources, targets)]
    copies = [pltpu.make_async_copy(a, b, sems.at[n]) for n, (a, b) in enumerate(zip(sources, targets))]
    for copy in copies:
        copy.start()
    size_x, size_y, lanes = out.shape
    receivers = amounts.shape[1]
    sublane = lax.broadcasted_iota(jnp.int32, (8, receivers), 0)
    at_depth = sublane == places[2]
    spread = [jnp.where(at_depth, amounts[t : t + 1], 0.0) for t in range(STEPS)]
    spread = jnp.concatenate(spread, axis=0)
    high = spread.astype(BF16).astype(F32)
    rest = spread - high
    middle = rest.astype(BF16).astype(F32)
    pieces = [high, middle, rest - middle, jnp.zeros_like(high)]
    weights[...] = jnp.concatenate(pieces, axis=0).T.astype(BF16)
    block = 8
    scale = openness[0, 0].astype(F32)
    lane = lax.broadcasted_iota(jnp.int32, (block * size_y, lanes), 1)
    local_x = places[0] - corner[0]
    rows = lax.broadcasted_iota(jnp.int32, (size_y, receivers), 0)
    at_y = jnp.where(rows == places[1] - corner[1], 1.0, 0.0).astype(BF16)

    def body(i, carry):
        hits = []
        for j in range(block):
            at_x = jnp.where(local_x == i * block + j, 1.0, 0.0).astype(BF16)
            hits.append(at_y * at_x)
        found = dot(jnp.concatenate(hits, axis=0), weights[...])
        found = found + pltpu.roll(found, lanes - 32, 1) + pltpu.roll(found, lanes - 64, 1)
        found = jnp.where(lane < 32, found * scale, 0.0)
        for j in range(block):
            out[i * block + j] = found[j * size_y : (j + 1) * size_y]
        return carry

    lax.fori_loop(0, size_x // block, body, 0)
    for copy in copies:
        copy.wait()


def make_coefficients(base, count, plane, r, ya, yb, ymat, zmat, ys, zs, stiff, buoy, coef, scale):
    size_y = r["size_y"]
    pairs = buoy.shape[0] // 2
    along_z = []
    for g in range(count):
        high, low = parts(buoy[base + g])
        if g % 2 == 0:
            hh, hl = halo_parts(ya, yb, pairs + (base + g) // 2)
        ys[g, 0:size_y] = dot(ymat[r["variant"] + g % 2, size_y:], jnp.concatenate([high, low, hh, hl], axis=0))
        along_z.append(jnp.concatenate([high, low], axis=1))
        if len(along_z) == 4:
            found = dot(jnp.concatenate(along_z, axis=0), zmat[:, 256:])
            zs[g - 3 : g + 1, :, 0:256] = found.reshape(4, size_y, 256)
            along_z = []
    for row in range(0, size_y, 16):
        for lane in range(0, 256, 128):
            at = (slice(row, row + 16), slice(lane, lane + 128))
            window = [plane(j, at) for j in range(count + 2 * RADIUS)]
            for g in range(count):
                s = stiff[(base + g,) + at] * scale
                t = s * (1.0 / (FIRST_SCALE * FIRST_SCALE))
                coef[0][(base + g,) + at] = s * (1.0 / SECOND_SCALE) * window[g + RADIUS]
                coef[1][(base + g,) + at] = t * x_first(window, g)
                coef[2][(base + g,) + at] = t * ys[(g,) + at]
                coef[3][(base + g,) + at] = t * zs[(g,) + at]


def advance(base, count, plane, r, step, q, p, out, ya, yb, ymat, zmat, ys, zs, coef, inject, snap, image, scale):
    size_y = r["size_y"]
    for g in range(count):
        high, low = parts(q[base + g])
        if g % 2 == 0:
            hh, hl = halo_parts(ya, yb, (base + g) // 2)
        ys[g] = dot(ymat[r["variant"] + g % 2], jnp.concatenate([high, low, hh, hl], axis=0))
        zs[g] = dot(jnp.concatenate([high, low], axis=1), zmat[...])
    elementwise(base, count, plane, r, step, q, p, out, ys, zs, coef, inject, snap, image, scale)


def elementwise(base, count, plane, r, step, q, p, out, ys, zs, coef, inject, snap, image, scale):
    size_y = r["size_y"]
    for row in range(0, size_y, 16):
        for lane in range(0, 256, 128):
            at = (slice(row, row + 16), slice(lane, lane + 128))
            below = (slice(size_y + row, size_y + row + 16), slice(lane, lane + 128))
            beside = (slice(row, row + 16), slice(256 + lane, 256 + lane + 128))
            window = [plane(j, at) for j in range(count + 2 * RADIUS)]
            for g in range(count):
                here = (base + g,) + at
                centre = window[g + RADIUS]
                second, first = x_both(window, g)
                second = second + (ys[(g,) + at] + zs[(g,) + at])
                change = coef[0][here] * second + coef[1][here] * first
                change = change + coef[2][here] * ys[(g,) + below] + coef[3][here] * zs[(g,) + beside]
                kept = (centre + centre) - p[here]
                if step < 2:
                    kept = kept * scale
                if lane == 0:
                    added = pltpu.roll(inject[base + g, row : row + 16, :], (128 - 8 * step) % 128, 1)
                    depth = lax.broadcasted_iota(jnp.int32, (16, 128), 1)
                    kept = kept + jnp.where(depth < 8, added, 0.0)
                value = kept + change
                out[here] = value
                shown = snap[here].astype(F32) * value
                image[here] = shown if step == 0 else image[here] + shown


def mute(image, source, corner, ranges):
    size_y = image.shape[1]
    y = lax.broadcasted_iota(jnp.int32, (size_y, 128), 0) + corner[1] - source[0, 1]
    z = lax.broadcasted_iota(jnp.int32, (size_y, 128), 1) - source[0, 2]
    flat = y * y + z * z
    for dx in range(1 - MUTE, MUTE):
        at = source[0, 0] - corner[0] + dx
        inside = functools.reduce(lambda a, b: a | b, [(at >= lo) & (at < hi) for lo, hi in ranges])

        @pl.when(inside)
        def _():
            image[at, :, 0:128] = jnp.where(flat + dx * dx < MUTE * MUTE, 0.0, image[at, :, 0:128])


def split_image(image, sent, kept, core, ranges):
    (lower, _), (upper, _) = ranges

    def body(i, carry):
        sent[i] = image[jnp.where(core == 0, upper, lower) + i]
        kept[i] = image[jnp.where(core == 0, lower, upper) + i]
        return carry

    lax.fori_loop(0, sent.shape[0], body, 0)


def step_kernel(step, ranges, edges, splits, names, *refs):
    r = dict(zip(names, refs))
    q, corner = r["q"], r["corner"]
    size_x, size_y, _ = q.shape
    r["size_y"] = size_y
    r["variant"] = 2 * corner[4]
    scale = r["openness"][0, 0].astype(F32)
    coef = [r["c%d" % i] for i in range(4)]
    common = (r["ya"], r["yb"], r["ymat"], r["zmat"], r["ys"], r["zs"])
    if "snap_next" in r:
        copy = pltpu.make_async_copy(r["snaps"].at[step + 1], r["snap_next"], r["sem"])
        copy.start()

    def inflow(start, size, n):
        pairs = ((r["p_far"], r["p"]), (r["stiff_far"], r["stiff"]))
        at = pl.ds(start, size)
        return [pltpu.make_async_copy(a.at[at], b.at[at], r["sems"].at[k, n]) for k, (a, b) in enumerate(pairs)]

    arriving = []
    if "sems" in r:
        low, high = ranges[0]
        groups = (high - low) // G
        for i in range(groups):
            arriving += inflow(low + i * G, G, i)
        arriving += inflow(0, RADIUS, groups) + inflow(high, RADIUS, groups + 1)
        for copy_in in arriving:
            copy_in.start()

    def reader(field, base, offset):
        def plane(j, at):
            where = base - RADIUS + j
            if isinstance(where, int) and where < 0:
                return r["halo"][(0, offset + where + RADIUS) + at]
            if isinstance(where, int) and where >= size_x:
                return r["halo"][(1, offset + where - size_x) + at]
            return field[(where,) + at]

        return plane

    def group(base, count):
        if step == 0:
            make_coefficients(
                base, count, reader(r["buoy"], base, RADIUS), r, *common, r["stiff"], r["buoy"], coef, scale
            )
        advance(
            base, count, reader(q, base, 0), r, step, q, r["p"], r["out"], *common, coef, r["inject"], r["snap"],
            r["image"], scale
        )

    for low, high in ranges:
        count = G if (high - low) % G == 0 else 4

        def body(i, carry):
            if arriving:
                for copy_in in inflow(low + i * count, count, i):
                    copy_in.wait()
            group(low + i * count, count)
            return carry

        lax.fori_loop(0, (high - low) // count, body, 0)
    for copy_in in arriving[-4:]:
        copy_in.wait()
    if edges:
        r["halo"][corner[3]] = r["xa"][...]
        r["halo"][1 - corner[3]] = r["xb"][...]
        group(0, RADIUS)
        group(size_x - RADIUS, RADIUS)
        ranges = ranges + [(0, RADIUS), (size_x - RADIUS, size_x)]
    if step == STEPS - 1:
        mute(r["image"], r["source"], corner, ranges)
    if step == STEPS - 1:
        for n, halves in enumerate(splits):
            split_image(r["image"], r["sent%d" % n], r["kept%d" % n], corner[2], halves)
    elif edges:
        top = size_x - RADIUS
        r["sxa"][...] = r["out"][pl.ds(top * corner[3], RADIUS)]
        r["sxb"][...] = r["out"][pl.ds(top * (1 - corner[3]), RADIUS)]
        pack_strips(r["out"].at[:, 0:8], r["out"].at[:, size_y - 8 :], corner[4] == 1, r["sya"], r["syb"], 0)
    if "snap_next" in r:
        copy.wait()


def add_kernel(a, b, *rest):
    rest[-1][...] = a[...] + b[...]


def gather_kernel(splits, corner, *refs):
    out, sems = refs[-2:]
    core = corner[2]
    copies = []
    for n, ((lower, _), (upper, _)) in enumerate(splits):
        for k, (source, first, second) in enumerate(((refs[2 * n], lower, upper), (refs[2 * n + 1], upper, lower))):
            at = pl.ds(jnp.where(core == 0, first, second), source.shape[0])
            copies.append(pltpu.make_async_copy(source, out.at[at], sems.at[n, k]))
    for copy in copies:
        copy.start()
    for copy in copies:
        copy.wait()


def store_kernel(source, out, sem):
    copy = pltpu.make_async_copy(source, out, sem)
    copy.start()
    copy.wait()


VMEM = pl.BlockSpec(memory_space=pltpu.VMEM)
SMEM = pl.BlockSpec(memory_space=pltpu.SMEM)
HBM = pl.BlockSpec(memory_space=pltpu.HBM)


def placed(args, specs):
    return [a if s is SMEM else pltpu.with_memory_space_constraint(a, s.memory_space) for a, s in zip(args, specs)]


def call(kernel, name, args, specs, outs, aliases={}, scratch=(), weight=1):
    outs = [pltpu.VMEM(o, F32) if isinstance(o, tuple) else o for o in outs]
    results = pl.pallas_call(
        kernel,
        name=name,
        in_specs=specs,
        out_specs=[pl.BlockSpec(memory_space=o.memory_space) for o in outs],
        out_shape=outs,
        input_output_aliases=aliases,
        scratch_shapes=list(scratch),
        compiler_params=pltpu.CompilerParams(vmem_limit_bytes=8 << 20),
        cost_estimate=pl.CostEstimate(flops=weight, bytes_accessed=1, transcendentals=0),
    )(*placed(args, specs))
    return list(results)


def exchange(strips):
    sxa, sxb, sya, syb = strips

    def swap(strip, stride, odd):
        tiles = range(lax.axis_size("dom"))
        position = lambda i: i % 4 if stride == 1 else i // 4
        last = 3 if stride == 1 else len(tiles) // 4 - 1
        pairs = [(i, i + stride) for i in tiles if position(i) % 2 == odd and position(i) < last]
        return lax.ppermute(strip, "dom", pairs + [(b, a) for a, b in pairs])

    ya, yb = swap(sya, 1, 0), swap(syb, 1, 1)
    xa, xb = swap(sxa, 4, 1), swap(sxb, 4, 0)
    return xa, xb, ya, yb


CORES = [(i, i ^ 1) for i in range(4)]
CHIPS = [(i, i ^ 2) for i in range(4)]


def add_cores(sent, kept):
    arrived = lax.ppermute(sent, "shot", CORES)
    return call(add_kernel, "add_cores", (kept, arrived), [VMEM] * 2, [kept.shape])[0]


def add_chips(mine, after):
    arrived = lax.ppermute(mine, "shot", CHIPS)
    args, specs = [mine, arrived] + after, [VMEM] * 2 + [HBM] * len(after)
    (mine,) = call(add_kernel, "add_chips", args, specs, [mine.shape])
    return mine, lax.ppermute(mine, "shot", CORES)


def on_device(wave_prev, wave_now, stiffness, buoyancy, snapshots, traces, aperture, receivers, sources):
    index = lax.axis_index("dom")
    size_x, size_y, size_z = grid = buoyancy.shape[1:]
    corner = [index // 4 * size_x, index % 4 * size_y, lax.axis_index("shot") % 2, index // 4 % 2, index % 2]
    corner = jnp.stack(corner).astype(jnp.int32)
    places = receivers[0].T[:, None, :]
    ymat, zmat = jnp.asarray(y_matrices(size_y)), jnp.asarray(z_matrix(size_z))
    snaps = snapshots[0, :, 0]

    strips = call(
        strips_kernel, "strips", (wave_now[0, 0], buoyancy[0], corner), [HBM, HBM, SMEM],
        [(2 * RADIUS, size_y, size_z)] * 2 + [(size_x, 8, size_z)] * 2,
        scratch=[pltpu.VMEM((2, 2, size_x, 8, size_z), F32), pltpu.SemaphoreType.DMA((8,))],
    )
    halos = exchange(strips)
    fetched = [wave_now[0, 0], buoyancy[0], ymat, zmat, snaps]
    shapes = [a.shape for a in fetched[:-1]] + [grid]
    args = [places, traces[0], aperture, corner] + fetched
    inject, q, buoy, ymat, zmat, snap = call(
        fetch_kernel, "fetch", args, [VMEM, VMEM, SMEM, SMEM] + [HBM] * len(fetched),
        [(size_x, size_y, 128)] + [pltpu.VMEM(shape, a.dtype) for shape, a in zip(shapes, fetched)],
        scratch=[pltpu.VMEM((traces.shape[2], 128), BF16), pltpu.SemaphoreType.DMA((len(fetched),))],
    )

    held = dict(inject=inject, ymat=ymat, zmat=zmat, openness=aperture, source=sources, corner=corner, snaps=snaps)
    held.update(q=q, buoy=buoy, snap=snap, p_far=wave_prev[0, 0], stiff_far=stiffness[0])
    places_of = dict(openness=SMEM, source=SMEM, corner=SMEM, snaps=HBM, p_far=HBM, stiff_far=HBM)

    def run(step, ranges, edges, started, extra, splits=(), weight=1):
        ahead = not edges and step < STEPS - 1
        fresh = step == 0 and not edges
        ins = ["q", "snap", "inject", "ya", "yb", "ymat", "zmat", "openness", "source", "corner"]
        ins += (["xa", "xb"] if edges else []) + (["snaps"] if ahead else [])
        ins += ["p_far", "stiff_far"] if fresh else ["p"]
        ins += ["buoy"] if step == 0 else ["c0", "c1", "c2", "c3"]
        ins += ["stiff"] if step == 0 and edges else []
        results = ["out", "image"] + (["c0", "c1", "c2", "c3"] if step == 0 else []) + (["p", "stiff"] if fresh else [])
        given = [n for n in results if n in started]
        extra = dict(extra)
        scratch = dict(
            ys=pltpu.VMEM((G, 2 * size_y, size_z), F32), zs=pltpu.VMEM((G, size_y, 2 * size_z), F32)
        )
        if ahead:
            extra["snap_next"] = pltpu.VMEM(grid, snaps.dtype)
            scratch["sem"] = pltpu.SemaphoreType.DMA
        if fresh:
            scratch["sems"] = pltpu.SemaphoreType.DMA((2, size_x // G + 1))
        if edges:
            scratch["halo"] = pltpu.VMEM((2,) + held["xa"].shape, F32)
        names = ins + [n + "_in" for n in given] + results + list(extra) + list(scratch)
        outs = call(
            functools.partial(step_kernel, step, ranges, edges, splits, names), "step%d" % step,
            [held[n] for n in ins + given], [places_of.get(n, VMEM) for n in ins + given],
            [grid] * len(results) + list(extra.values()),
            {len(ins) + i: results.index(n) for i, n in enumerate(given)}, scratch.values(), weight,
        )
        held.update(zip(results, outs))
        return outs[len(results) :]

    inner = [(RADIUS, size_x - RADIUS)]
    strip_x, strip_y = (RADIUS, size_y, size_z), (size_x // 2, 8, size_z)
    first = ("out", "image", "c0", "c1", "c2", "c3")
    for step in range(STEPS - 1):
        held.update(zip(("xa", "xb", "ya", "yb"), halos))
        (snap_next,) = run(step, inner, False, ("image",) if step else (), {}, weight=4 << 30)
        extra = dict(sxa=strip_x, sxb=strip_x, sya=strip_y, syb=strip_y)
        halos = exchange(run(step, [], True, first if step == 0 else ("out", "image"), extra))
        held.update(q=held["out"], p=held["q"], snap=snap_next)

    held.update(zip(("xa", "xb", "ya", "yb"), halos))
    run(STEPS - 1, inner, False, ("image",), {}, weight=4 << 30)
    splits, halves, at = [], {}, 0
    for i, size in enumerate((4, 8, 8, 4)):
        splits.append(((at, at + size), (size_x - at - size, size_x - at)))
        halves.update({"sent%d" % i: (size, size_y, size_z), "kept%d" % i: (size, size_y, size_z)})
        at += size
    halves = run(STEPS - 1, [], True, ("out", "image"), halves, splits)
    sums = [add_cores(*halves[2 * i : 2 * i + 2]) for i in range(len(splits))]
    (last,) = call(store_kernel, "store", [held["out"]], [VMEM], [pltpu.HBM(grid, F32)], {}, [pltpu.SemaphoreType.DMA])
    started, chunks = [], []
    for n, mine in enumerate(sums):
        chunks += add_chips(mine, started + [last] if n == 3 else [])
        if n % 2:
            ranges = splits[n - 1 : n + 1]
            started = call(
                functools.partial(gather_kernel, ranges), "gather", [corner] + chunks + started,
                [SMEM] + [VMEM] * 4 + [HBM] * len(started), [pltpu.HBM(grid, F32)], {5: 0} if started else {},
                [pltpu.SemaphoreType.DMA((2, 2))],
            )
            chunks = []
    return started[0][None], last[None, None]


def solution(mesh):
    return jax.shard_map(
        on_device,
        mesh=mesh,
        in_specs=(
            P("shot", "dom", None, None, None),
            P("shot", "dom", None, None, None),
            P("dom", None, None, None),
            P("dom", None, None, None),
            P("shot", None, "dom", None, None, None),
            P("shot", None, None),
            P("shot", "dom"),
            P("shot", None, None),
            P("shot", None),
        ),
        out_specs=(P("dom", None, None, None), P("shot", "dom", None, None, None)),
        check_vma=False,
    )
```

```python
import functools

import jax
import jax.numpy as jnp
import ml_dtypes
import numpy as np
from jax import lax
from jax.experimental import pallas as pl
from jax.experimental.pallas import tpu as pltpu
from jax.sharding import PartitionSpec as P

STEPS = 4
MUTE = 6
G = 8
RADIUS = 4

SECOND = (63.0, -7.875, 1.0, -0.0703125)
SECOND_CENTRE_Y, SECOND_CENTRE_Z = -336.0, -0.328125
SECOND_SCALE = 5040.0 / 128.0
FIRST = (21.0, -5.25, 1.0, -0.09375)
FIRST_SCALE = 840.0 / 32.0

F32 = jnp.float32
BF16 = jnp.bfloat16


def banded(size, weights, odd, centre=0.0):
    matrix = np.zeros((size, size + 2 * RADIUS), np.float32)
    for i in range(size):
        matrix[i, i + RADIUS] = centre
        for k, w in enumerate(weights, 1):
            matrix[i, i + RADIUS + k] = w
            matrix[i, i + RADIUS - k] = -w if odd else w
    return matrix


def y_matrices(size):
    both = np.concatenate([banded(size, SECOND, False, SECOND_CENTRE_Y), banded(size, FIRST, True)])
    own = both[:, RADIUS:-RADIUS]
    result = []
    for tile, parity in ((0, 0), (0, 1), (1, 0), (1, 1)):
        below, above = 8 * (1 - tile) + 4 * parity, 8 * tile + 4 * parity
        halo = np.zeros((2 * size, 16), np.float32)
        halo[:, below : below + 4] = both[:, :RADIUS]
        halo[:, above : above + 4] = both[:, -RADIUS:]
        result.append(np.concatenate([own, own, halo, halo], axis=1))
    return np.stack(result).astype(ml_dtypes.bfloat16)


def z_matrix(size):
    second = banded(size, SECOND, False, SECOND_CENTRE_Z)[:, RADIUS:-RADIUS].T
    first = banded(size, FIRST, True)[:, RADIUS:-RADIUS].T
    both = np.concatenate([second, first], axis=1)
    return np.concatenate([both, both], axis=0).astype(ml_dtypes.bfloat16)


def parts(value):
    high = value.astype(BF16)
    low = (value - high.astype(F32)).astype(BF16)
    return high, low


def dot(a, b):
    return jnp.dot(a, b, preferred_element_type=F32)


def weighted(weights, terms):
    terms = [t if w == 1.0 else w * t for w, t in zip(weights, terms)]
    return functools.reduce(lambda a, b: a + b, terms)


def x_first(window, g):
    return weighted(FIRST, [window[g + RADIUS + k] - window[g + RADIUS - k] for k in range(1, RADIUS + 1)])


def x_second(window, g):
    return weighted(SECOND, [window[g + RADIUS + k] + window[g + RADIUS - k] for k in range(1, RADIUS + 1)])


def halo_parts(first_ref, second_ref, pair):
    return parts(jnp.concatenate([first_ref[pair], second_ref[pair]], axis=0))


def pack_strips(lowest, highest, odd_tile, first_ref, second_ref, offset):
    rows = lax.broadcasted_iota(jnp.int32, lowest.shape[1:], 0)

    def body(i, carry):
        even, odd = lowest[2 * i], lowest[2 * i + 1]
        low = jnp.where(rows < 4, even, pltpu.roll(odd, 4, 0))
        even, odd = highest[2 * i], highest[2 * i + 1]
        high = jnp.where(rows < 4, pltpu.roll(even, 4, 0), odd)
        first_ref[offset + i] = jnp.where(odd_tile, low, high)
        second_ref[offset + i] = jnp.where(odd_tile, high, low)
        return carry

    lax.fori_loop(0, lowest.shape[0] // 2, body, 0, unroll=4)


def strips_kernel(q, b, corner, xa, xb, ya, yb, rows, sems):
    size_x, size_y, _ = q.shape
    top = size_x - RADIUS
    copies = []
    for i, source in enumerate((q, b)):
        at = RADIUS * i
        copies += [
            (source.at[:, 0:8], rows.at[i, 0]),
            (source.at[:, size_y - 8 : size_y], rows.at[i, 1]),
            (source.at[pl.ds(top * corner[3], RADIUS)], xa.at[at : at + RADIUS]),
            (source.at[pl.ds(top * (1 - corner[3]), RADIUS)], xb.at[at : at + RADIUS]),
        ]
    copies = [pltpu.make_async_copy(*pair, sems.at[n]) for n, pair in enumerate(copies)]
    for copy in copies:
        copy.start()
    for i in range(2):
        copies[4 * i].wait()
        copies[4 * i + 1].wait()
        pack_strips(rows.at[i, 0], rows.at[i, 1], corner[4] == 1, ya, yb, i * (size_x // 2))
    for i in range(2):
        copies[4 * i + 2].wait()
        copies[4 * i + 3].wait()


def fetch_kernel(places, amounts, openness, corner, *refs):
    count = (len(refs) - 3) // 2
    sources, targets = refs[:count], refs[count + 1 : 2 * count + 1]
    out, (weights, sems) = refs[count], refs[2 * count + 1 :]
    sources = [a if a.shape == b.shape else a.at[0] for a, b in zip(sources, targets)]
    copies = [pltpu.make_async_copy(a, b, sems.at[n]) for n, (a, b) in enumerate(zip(sources, targets))]
    for copy in copies:
        copy.start()
    size_x, size_y, lanes = out.shape
    receivers = amounts.shape[1]
    sublane = lax.broadcasted_iota(jnp.int32, (8, receivers), 0)
    at_depth = sublane == places[2]
    spread = [jnp.where(at_depth, amounts[t : t + 1], 0.0) for t in range(STEPS)]
    spread = jnp.concatenate(spread, axis=0)
    high = spread.astype(BF16).astype(F32)
    rest = spread - high
    middle = rest.astype(BF16).astype(F32)
    pieces = [high, middle, rest - middle, jnp.zeros_like(high)]
    weights[...] = jnp.concatenate(pieces, axis=0).T.astype(BF16)
    block = 8
    scale = openness[0, 0].astype(F32)
    lane = lax.broadcasted_iota(jnp.int32, (block * size_y, lanes), 1)
    local_x = places[0] - corner[0]
    rows = lax.broadcasted_iota(jnp.int32, (size_y, receivers), 0)
    at_y = jnp.where(rows == places[1] - corner[1], 1.0, 0.0).astype(BF16)

    def body(i, carry):
        hits = []
        for j in range(block):
            at_x = jnp.where(local_x == i * block + j, 1.0, 0.0).astype(BF16)
            hits.append(at_y * at_x)
        found = dot(jnp.concatenate(hits, axis=0), weights[...])
        found = found + pltpu.roll(found, lanes - 32, 1) + pltpu.roll(found, lanes - 64, 1)
        found = jnp.where(lane < 32, found * scale, 0.0)
        for j in range(block):
            out[i * block + j] = found[j * size_y : (j + 1) * size_y]
        return carry

    lax.fori_loop(0, size_x // block, body, 0)
    for copy in copies:
        copy.wait()


def make_coefficients(base, count, plane, r, ya, yb, ymat, zmat, ys, zs, stiff, buoy, coef, scale):
    size_y = r["size_y"]
    pairs = buoy.shape[0] // 2
    along_z = []
    for g in range(count):
        high, low = parts(buoy[base + g])
        if g % 2 == 0:
            hh, hl = halo_parts(ya, yb, pairs + (base + g) // 2)
        ys[g, 0:size_y] = dot(ymat[r["variant"] + g % 2, size_y:], jnp.concatenate([high, low, hh, hl], axis=0))
        along_z.append(jnp.concatenate([high, low], axis=1))
        if len(along_z) == 4:
            found = dot(jnp.concatenate(along_z, axis=0), zmat[:, 256:])
            zs[g - 3 : g + 1, :, 0:256] = found.reshape(4, size_y, 256)
            along_z = []
    for row in range(0, size_y, 16):
        for lane in range(0, 256, 128):
            at = (slice(row, row + 16), slice(lane, lane + 128))
            window = [plane(j, at) for j in range(count + 2 * RADIUS)]
            for g in range(count):
                s = stiff[(base + g,) + at] * scale
                t = s * (1.0 / (FIRST_SCALE * FIRST_SCALE))
                coef[0][(base + g,) + at] = s * (1.0 / SECOND_SCALE) * window[g + RADIUS]
                coef[1][(base + g,) + at] = t * x_first(window, g)
                coef[2][(base + g,) + at] = t * ys[(g,) + at]
                coef[3][(base + g,) + at] = t * zs[(g,) + at]


def advance(base, count, plane, r, step, q, p, out, ya, yb, ymat, zmat, ys, zs, coef, inject, snap, image, scale):
    size_y = r["size_y"]
    for g in range(count):
        high, low = parts(q[base + g])
        if g % 2 == 0:
            hh, hl = halo_parts(ya, yb, (base + g) // 2)
        ys[g] = dot(ymat[r["variant"] + g % 2], jnp.concatenate([high, low, hh, hl], axis=0))
        zs[g] = dot(jnp.concatenate([high, low], axis=1), zmat[...])
    elementwise(base, count, plane, r, step, q, p, out, ys, zs, coef, inject, snap, image, scale)


def elementwise(base, count, plane, r, step, q, p, out, ys, zs, coef, inject, snap, image, scale):
    size_y = r["size_y"]
    for row in range(0, size_y, 16):
        for lane in range(0, 256, 128):
            at = (slice(row, row + 16), slice(lane, lane + 128))
            below = (slice(size_y + row, size_y + row + 16), slice(lane, lane + 128))
            beside = (slice(row, row + 16), slice(256 + lane, 256 + lane + 128))
            window = [plane(j, at) for j in range(count + 2 * RADIUS)]
            for g in range(count):
                here = (base + g,) + at
                centre = window[g + RADIUS]
                first = x_first(window, g)
                second = x_second(window, g) + (ys[(g,) + at] + zs[(g,) + at])
                change = coef[0][here] * second + coef[1][here] * first
                change = change + coef[2][here] * ys[(g,) + below] + coef[3][here] * zs[(g,) + beside]
                kept = (centre + centre) - p[here]
                if step < 2:
                    kept = kept * scale
                if lane == 0:
                    added = pltpu.roll(inject[base + g, row : row + 16, :], (128 - 8 * step) % 128, 1)
                    depth = lax.broadcasted_iota(jnp.int32, (16, 128), 1)
                    kept = kept + jnp.where(depth < 8, added, 0.0)
                value = kept + change
                out[here] = value
                shown = snap[here].astype(F32) * value
                image[here] = shown if step == 0 else image[here] + shown


def mute(image, source, corner, ranges):
    size_y = image.shape[1]
    y = lax.broadcasted_iota(jnp.int32, (size_y, 128), 0) + corner[1] - source[0, 1]
    z = lax.broadcasted_iota(jnp.int32, (size_y, 128), 1) - source[0, 2]
    flat = y * y + z * z
    for dx in range(1 - MUTE, MUTE):
        at = source[0, 0] - corner[0] + dx
        inside = functools.reduce(lambda a, b: a | b, [(at >= lo) & (at < hi) for lo, hi in ranges])

        @pl.when(inside)
        def _():
            image[at, :, 0:128] = jnp.where(flat + dx * dx < MUTE * MUTE, 0.0, image[at, :, 0:128])


def split_image(image, sent, kept, core, ranges):
    (lower, _), (upper, _) = ranges

    def body(i, carry):
        sent[i] = image[jnp.where(core == 0, upper, lower) + i]
        kept[i] = image[jnp.where(core == 0, lower, upper) + i]
        return carry

    lax.fori_loop(0, sent.shape[0], body, 0)


def step_kernel(step, ranges, edges, splits, names, *refs):
    r = dict(zip(names, refs))
    q, corner = r["q"], r["corner"]
    size_x, size_y, _ = q.shape
    r["size_y"] = size_y
    r["variant"] = 2 * corner[4]
    scale = r["openness"][0, 0].astype(F32)
    coef = [r["c%d" % i] for i in range(4)]
    common = (r["ya"], r["yb"], r["ymat"], r["zmat"], r["ys"], r["zs"])
    if "snap_next" in r:
        copy = pltpu.make_async_copy(r["snaps"].at[step + 1], r["snap_next"], r["sem"])
        copy.start()

    def inflow(start, size, n):
        pairs = ((r["p_far"], r["p"]), (r["stiff_far"], r["stiff"]))
        at = pl.ds(start, size)
        return [pltpu.make_async_copy(a.at[at], b.at[at], r["sems"].at[k, n]) for k, (a, b) in enumerate(pairs)]

    arriving = []
    if "sems" in r:
        low, high = ranges[0]
        groups = (high - low) // G
        for i in range(groups):
            arriving += inflow(low + i * G, G, i)
        arriving += inflow(0, RADIUS, groups) + inflow(high, RADIUS, groups + 1)
        for copy_in in arriving:
            copy_in.start()

    def reader(field, base, offset):
        def plane(j, at):
            where = base - RADIUS + j
            if isinstance(where, int) and where < 0:
                return r["halo"][(0, offset + where + RADIUS) + at]
            if isinstance(where, int) and where >= size_x:
                return r["halo"][(1, offset + where - size_x) + at]
            return field[(where,) + at]

        return plane

    def group(base, count):
        if step == 0:
            make_coefficients(
                base, count, reader(r["buoy"], base, RADIUS), r, *common, r["stiff"], r["buoy"], coef, scale
            )
        advance(
            base, count, reader(q, base, 0), r, step, q, r["p"], r["out"], *common, coef, r["inject"], r["snap"],
            r["image"], scale
        )

    for low, high in ranges:
        count = G if (high - low) % G == 0 else 4

        def body(i, carry):
            if arriving:
                for copy_in in inflow(low + i * count, count, i):
                    copy_in.wait()
            group(low + i * count, count)
            return carry

        lax.fori_loop(0, (high - low) // count, body, 0)
    for copy_in in arriving[-4:]:
        copy_in.wait()
    if edges:
        r["halo"][corner[3]] = r["xa"][...]
        r["halo"][1 - corner[3]] = r["xb"][...]
        group(0, RADIUS)
        group(size_x - RADIUS, RADIUS)
        ranges = ranges + [(0, RADIUS), (size_x - RADIUS, size_x)]
    if step == STEPS - 1:
        mute(r["image"], r["source"], corner, ranges)
    if step == STEPS - 1:
        for n, halves in enumerate(splits):
            split_image(r["image"], r["sent%d" % n], r["kept%d" % n], corner[2], halves)
    elif edges:
        top = size_x - RADIUS
        r["sxa"][...] = r["out"][pl.ds(top * corner[3], RADIUS)]
        r["sxb"][...] = r["out"][pl.ds(top * (1 - corner[3]), RADIUS)]
        pack_strips(r["out"].at[:, 0:8], r["out"].at[:, size_y - 8 :], corner[4] == 1, r["sya"], r["syb"], 0)
    if "snap_next" in r:
        copy.wait()


def add_kernel(a, b, *rest):
    rest[-1][...] = a[...] + b[...]


def gather_kernel(splits, corner, *refs):
    out, sems = refs[-2:]
    core = corner[2]
    copies = []
    for n, ((lower, _), (upper, _)) in enumerate(splits):
        for k, (source, first, second) in enumerate(((refs[2 * n], lower, upper), (refs[2 * n + 1], upper, lower))):
            at = pl.ds(jnp.where(core == 0, first, second), source.shape[0])
            copies.append(pltpu.make_async_copy(source, out.at[at], sems.at[n, k]))
    for copy in copies:
        copy.start()
    for copy in copies:
        copy.wait()


def store_kernel(source, out, sem):
    copy = pltpu.make_async_copy(source, out, sem)
    copy.start()
    copy.wait()


VMEM = pl.BlockSpec(memory_space=pltpu.VMEM)
SMEM = pl.BlockSpec(memory_space=pltpu.SMEM)
HBM = pl.BlockSpec(memory_space=pltpu.HBM)


def placed(args, specs):
    return [a if s is SMEM else pltpu.with_memory_space_constraint(a, s.memory_space) for a, s in zip(args, specs)]


def call(kernel, name, args, specs, outs, aliases={}, scratch=(), weight=1):
    outs = [pltpu.VMEM(o, F32) if isinstance(o, tuple) else o for o in outs]
    results = pl.pallas_call(
        kernel,
        name=name,
        in_specs=specs,
        out_specs=[pl.BlockSpec(memory_space=o.memory_space) for o in outs],
        out_shape=outs,
        input_output_aliases=aliases,
        scratch_shapes=list(scratch),
        compiler_params=pltpu.CompilerParams(vmem_limit_bytes=8 << 20),
        cost_estimate=pl.CostEstimate(flops=weight, bytes_accessed=1, transcendentals=0),
    )(*placed(args, specs))
    return list(results)


def exchange(strips):
    sxa, sxb, sya, syb = strips

    def swap(strip, stride, odd):
        tiles = range(lax.axis_size("dom"))
        position = lambda i: i % 4 if stride == 1 else i // 4
        last = 3 if stride == 1 else len(tiles) // 4 - 1
        pairs = [(i, i + stride) for i in tiles if position(i) % 2 == odd and position(i) < last]
        return lax.ppermute(strip, "dom", pairs + [(b, a) for a, b in pairs])

    ya, yb = swap(sya, 1, 0), swap(syb, 1, 1)
    xa, xb = swap(sxa, 4, 1), swap(sxb, 4, 0)
    return xa, xb, ya, yb


CORES = [(i, i ^ 1) for i in range(4)]
CHIPS = [(i, i ^ 2) for i in range(4)]


def add_cores(sent, kept, after=()):
    arrived = lax.ppermute(sent, "shot", CORES)
    args = [kept, arrived] + list(after)
    return call(add_kernel, "add_cores", args, [VMEM] * len(args), [kept.shape])[0]


def add_chips(mine, after):
    arrived = lax.ppermute(mine, "shot", CHIPS)
    args, specs = [mine, arrived] + after, [VMEM] * 2 + [HBM] * len(after)
    (mine,) = call(add_kernel, "add_chips", args, specs, [mine.shape])
    return mine, lax.ppermute(mine, "shot", CORES)


def on_device(wave_prev, wave_now, stiffness, buoyancy, snapshots, traces, aperture, receivers, sources):
    index = lax.axis_index("dom")
    size_x, size_y, size_z = grid = buoyancy.shape[1:]
    corner = [index // 4 * size_x, index % 4 * size_y, lax.axis_index("shot") % 2, index // 4 % 2, index % 2]
    corner = jnp.stack(corner).astype(jnp.int32)
    places = receivers[0].T[:, None, :]
    ymat, zmat = jnp.asarray(y_matrices(size_y)), jnp.asarray(z_matrix(size_z))
    snaps = snapshots[0, :, 0]

    strips = call(
        strips_kernel, "strips", (wave_now[0, 0], buoyancy[0], corner), [HBM, HBM, SMEM],
        [(2 * RADIUS, size_y, size_z)] * 2 + [(size_x, 8, size_z)] * 2,
        scratch=[pltpu.VMEM((2, 2, size_x, 8, size_z), F32), pltpu.SemaphoreType.DMA((8,))],
    )
    halos = exchange(strips)
    fetched = [wave_now[0, 0], buoyancy[0], ymat, zmat, snaps]
    shapes = [a.shape for a in fetched[:-1]] + [grid]
    args = [places, traces[0], aperture, corner] + fetched
    inject, q, buoy, ymat, zmat, snap = call(
        fetch_kernel, "fetch", args, [VMEM, VMEM, SMEM, SMEM] + [HBM] * len(fetched),
        [(size_x, size_y, 128)] + [pltpu.VMEM(shape, a.dtype) for shape, a in zip(shapes, fetched)],
        scratch=[pltpu.VMEM((traces.shape[2], 128), BF16), pltpu.SemaphoreType.DMA((len(fetched),))],
    )

    held = dict(inject=inject, ymat=ymat, zmat=zmat, openness=aperture, source=sources, corner=corner, snaps=snaps)
    held.update(q=q, buoy=buoy, snap=snap, p_far=wave_prev[0, 0], stiff_far=stiffness[0])
    places_of = dict(openness=SMEM, source=SMEM, corner=SMEM, snaps=HBM, p_far=HBM, stiff_far=HBM)

    def run(step, ranges, edges, started, extra, splits=(), weight=1):
        ahead = not edges and step < STEPS - 1
        fresh = step == 0 and not edges
        ins = ["q", "snap", "inject", "ya", "yb", "ymat", "zmat", "openness", "source", "corner"]
        ins += (["xa", "xb"] if edges else []) + (["snaps"] if ahead else [])
        ins += ["p_far", "stiff_far"] if fresh else ["p"]
        ins += ["buoy"] if step == 0 else ["c0", "c1", "c2", "c3"]
        ins += ["stiff"] if step == 0 and edges else []
        results = ["out", "image"] + (["c0", "c1", "c2", "c3"] if step == 0 else []) + (["p", "stiff"] if fresh else [])
        given = [n for n in results if n in started]
        extra = dict(extra)
        scratch = dict(
            ys=pltpu.VMEM((G, 2 * size_y, size_z), F32), zs=pltpu.VMEM((G, size_y, 2 * size_z), F32)
        )
        if ahead:
            extra["snap_next"] = pltpu.VMEM(grid, snaps.dtype)
            scratch["sem"] = pltpu.SemaphoreType.DMA
        if fresh:
            scratch["sems"] = pltpu.SemaphoreType.DMA((2, size_x // G + 1))
        if edges:
            scratch["halo"] = pltpu.VMEM((2,) + held["xa"].shape, F32)
        names = ins + [n + "_in" for n in given] + results + list(extra) + list(scratch)
        outs = call(
            functools.partial(step_kernel, step, ranges, edges, splits, names), "step%d" % step,
            [held[n] for n in ins + given], [places_of.get(n, VMEM) for n in ins + given],
            [grid] * len(results) + list(extra.values()),
            {len(ins) + i: results.index(n) for i, n in enumerate(given)}, scratch.values(), weight,
        )
        held.update(zip(results, outs))
        return outs[len(results) :]

    inner = [(RADIUS, size_x - RADIUS)]
    strip_x, strip_y = (RADIUS, size_y, size_z), (size_x // 2, 8, size_z)
    first = ("out", "image", "c0", "c1", "c2", "c3")
    for step in range(STEPS - 1):
        held.update(zip(("xa", "xb", "ya", "yb"), halos))
        (snap_next,) = run(step, inner, False, ("image",) if step else (), {}, weight=4 << 30)
        extra = dict(sxa=strip_x, sxb=strip_x, sya=strip_y, syb=strip_y)
        halos = exchange(run(step, [], True, first if step == 0 else ("out", "image"), extra))
        held.update(q=held["out"], p=held["q"], snap=snap_next)

    held.update(zip(("xa", "xb", "ya", "yb"), halos))
    splits, at = [], 0
    for size in (8, 10, 6):
        splits.insert(0, ((at, at + size), (size_x - at - size, size_x - at)))
        at += size

    def halves(splits):
        shapes = [(lower[1] - lower[0], size_y, size_z) for lower, _ in splits]
        return {name + str(i): shape for i, shape in enumerate(shapes) for name in ("sent", "kept")}

    early = run(STEPS - 1, inner, False, ("image",), halves(splits[:1]), splits[:1], weight=4 << 30)
    late = run(STEPS - 1, [], True, ("out", "image"), halves(splits[1:]), splits[1:], weight=4 << 30)
    sums = [add_cores(*early, after=late[:1]), add_cores(*late[:2]), add_cores(*late[2:])]
    (last,) = call(store_kernel, "store", [held["out"]], [VMEM], [pltpu.HBM(grid, F32)], {}, [pltpu.SemaphoreType.DMA])
    def gather(splits, chunks, started):
        return call(
            functools.partial(gather_kernel, splits), "gather", [corner] + chunks + started,
            [SMEM] + [VMEM] * len(chunks) + [HBM] * len(started), [pltpu.HBM(grid, F32)],
            {1 + len(chunks): 0} if started else {}, [pltpu.SemaphoreType.DMA((len(splits), 2))],
        )

    started = gather(splits[:2], [*add_chips(sums[0], []), *add_chips(sums[1], [])], [])
    (gradient,) = gather(splits[2:], [*add_chips(sums[2], started + [last])], started)
    return gradient[None], last[None, None]


def solution(mesh):
    return jax.shard_map(
        on_device,
        mesh=mesh,
        in_specs=(
            P("shot", "dom", None, None, None),
            P("shot", "dom", None, None, None),
            P("dom", None, None, None),
            P("dom", None, None, None),
            P("shot", None, "dom", None, None, None),
            P("shot", None, None),
            P("shot", "dom"),
            P("shot", None, None),
            P("shot", None),
        ),
        out_specs=(P("dom", None, None, None), P("shot", "dom", None, None, None)),
        check_vma=False,
    )
```

```python
import functools

import jax
import jax.numpy as jnp
import ml_dtypes
import numpy as np
from jax import lax
from jax.experimental import pallas as pl
from jax.experimental.pallas import tpu as pltpu
from jax.sharding import PartitionSpec as P

STEPS = 4
MUTE = 6
G = 8
RADIUS = 4

SECOND = (63.0, -7.875, 1.0, -0.0703125)
SECOND_CENTRE_Y, SECOND_CENTRE_Z = -336.0, -0.328125
SECOND_SCALE = 5040.0 / 128.0
FIRST = (21.0, -5.25, 1.0, -0.09375)
FIRST_SCALE = 840.0 / 32.0

F32 = jnp.float32
BF16 = jnp.bfloat16


def banded(size, weights, odd, centre=0.0):
    matrix = np.zeros((size, size + 2 * RADIUS), np.float32)
    for i in range(size):
        matrix[i, i + RADIUS] = centre
        for k, w in enumerate(weights, 1):
            matrix[i, i + RADIUS + k] = w
            matrix[i, i + RADIUS - k] = -w if odd else w
    return matrix


def y_matrices(size):
    both = np.concatenate([banded(size, SECOND, False, SECOND_CENTRE_Y), banded(size, FIRST, True)])
    own = both[:, RADIUS:-RADIUS]
    result = []
    for tile, parity in ((0, 0), (0, 1), (1, 0), (1, 1)):
        below, above = 8 * (1 - tile) + 4 * parity, 8 * tile + 4 * parity
        halo = np.zeros((2 * size, 16), np.float32)
        halo[:, below : below + 4] = both[:, :RADIUS]
        halo[:, above : above + 4] = both[:, -RADIUS:]
        result.append(np.concatenate([own, own, halo, halo], axis=1))
    return np.stack(result).astype(ml_dtypes.bfloat16)


def z_matrix(size):
    second = banded(size, SECOND, False, SECOND_CENTRE_Z)[:, RADIUS:-RADIUS].T
    first = banded(size, FIRST, True)[:, RADIUS:-RADIUS].T
    both = np.concatenate([second, first], axis=1)
    return np.concatenate([both, both], axis=0).astype(ml_dtypes.bfloat16)


def parts(value):
    high = value.astype(BF16)
    low = (value - high.astype(F32)).astype(BF16)
    return high, low


def dot(a, b):
    return jnp.dot(a, b, preferred_element_type=F32)


def weighted(weights, terms):
    terms = [t if w == 1.0 else w * t for w, t in zip(weights, terms)]
    return functools.reduce(lambda a, b: a + b, terms)


def x_first(window, g):
    return weighted(FIRST, [window[g + RADIUS + k] - window[g + RADIUS - k] for k in range(1, RADIUS + 1)])


def x_second(window, g):
    return weighted(SECOND, [window[g + RADIUS + k] + window[g + RADIUS - k] for k in range(1, RADIUS + 1)])


def halo_parts(first_ref, second_ref, pair):
    return parts(jnp.concatenate([first_ref[pair], second_ref[pair]], axis=0))


def pack_strips(lowest, highest, odd_tile, first_ref, second_ref, offset):
    rows = lax.broadcasted_iota(jnp.int32, lowest.shape[1:], 0)

    def body(i, carry):
        even, odd = lowest[2 * i], lowest[2 * i + 1]
        low = jnp.where(rows < 4, even, pltpu.roll(odd, 4, 0))
        even, odd = highest[2 * i], highest[2 * i + 1]
        high = jnp.where(rows < 4, pltpu.roll(even, 4, 0), odd)
        first_ref[offset + i] = jnp.where(odd_tile, low, high)
        second_ref[offset + i] = jnp.where(odd_tile, high, low)
        return carry

    lax.fori_loop(0, lowest.shape[0] // 2, body, 0, unroll=8)


def strips_kernel(q, b, corner, xa, xb, ya, yb, rows, sems):
    size_x, size_y, _ = q.shape
    top = size_x - RADIUS
    copies = []
    for i, source in enumerate((q, b)):
        at = RADIUS * i
        copies += [
            (source.at[:, 0:8], rows.at[i, 0]),
            (source.at[:, size_y - 8 : size_y], rows.at[i, 1]),
            (source.at[pl.ds(top * corner[3], RADIUS)], xa.at[at : at + RADIUS]),
            (source.at[pl.ds(top * (1 - corner[3]), RADIUS)], xb.at[at : at + RADIUS]),
        ]
    copies = [pltpu.make_async_copy(*pair, sems.at[n]) for n, pair in enumerate(copies)]
    for copy in copies:
        copy.start()
    for i in range(2):
        copies[4 * i].wait()
        copies[4 * i + 1].wait()
        pack_strips(rows.at[i, 0], rows.at[i, 1], corner[4] == 1, ya, yb, i * (size_x // 2))
    for i in range(2):
        copies[4 * i + 2].wait()
        copies[4 * i + 3].wait()


def fetch_kernel(places, amounts, openness, corner, *refs):
    count = (len(refs) - 3) // 2
    sources, targets = refs[:count], refs[count + 1 : 2 * count + 1]
    out, (weights, sems) = refs[count], refs[2 * count + 1 :]
    pairs = list(zip(sources, targets))
    whole, (previous, stiff, snaps) = pairs[:-3], pairs[-3:]
    first = slice(0, RADIUS + G)
    pairs = whole + [(a.at[first], b.at[first]) for a, b in (previous, stiff, (snaps[0].at[0], snaps[1]))]
    copies = [pltpu.make_async_copy(a, b, sems.at[n]) for n, (a, b) in enumerate(pairs)]
    for copy in copies:
        copy.start()
    size_x, size_y, lanes = out.shape
    receivers = amounts.shape[1]
    sublane = lax.broadcasted_iota(jnp.int32, (8, receivers), 0)
    at_depth = sublane == places[2]
    spread = [jnp.where(at_depth, amounts[t : t + 1], 0.0) for t in range(STEPS)]
    spread = jnp.concatenate(spread, axis=0)
    high = spread.astype(BF16).astype(F32)
    rest = spread - high
    middle = rest.astype(BF16).astype(F32)
    pieces = [high, middle, rest - middle, jnp.zeros_like(high)]
    weights[...] = jnp.concatenate(pieces, axis=0).T.astype(BF16)
    block = 8
    scale = openness[0, 0].astype(F32)
    lane = lax.broadcasted_iota(jnp.int32, (block * size_y, lanes), 1)
    local_x = places[0] - corner[0]
    rows = lax.broadcasted_iota(jnp.int32, (size_y, receivers), 0)
    at_y = jnp.where(rows == places[1] - corner[1], 1.0, 0.0).astype(BF16)

    def body(i, carry):
        hits = []
        for j in range(block):
            at_x = jnp.where(local_x == i * block + j, 1.0, 0.0).astype(BF16)
            hits.append(at_y * at_x)
        found = dot(jnp.concatenate(hits, axis=0), weights[...])
        found = found + pltpu.roll(found, lanes - 32, 1) + pltpu.roll(found, lanes - 64, 1)
        found = jnp.where(lane < 32, found * scale, 0.0)
        for j in range(block):
            out[i * block + j] = found[j * size_y : (j + 1) * size_y]
        return carry

    lax.fori_loop(0, size_x // block, body, 0)
    for copy in copies:
        copy.wait()


def make_coefficients(base, count, plane, r, ya, yb, ymat, zmat, ys, zs, stiff, buoy, coef, scale):
    size_y = r["size_y"]
    pairs = buoy.shape[0] // 2
    along_z = []
    for g in range(count):
        high, low = parts(buoy[base + g])
        if g % 2 == 0:
            hh, hl = halo_parts(ya, yb, pairs + (base + g) // 2)
        ys[g, 0:size_y] = dot(ymat[r["variant"] + g % 2, size_y:], jnp.concatenate([high, low, hh, hl], axis=0))
        along_z.append(jnp.concatenate([high, low], axis=1))
        if len(along_z) == 4:
            found = dot(jnp.concatenate(along_z, axis=0), zmat[:, 256:])
            zs[g - 3 : g + 1, :, 0:256] = found.reshape(4, size_y, 256)
            along_z = []
    for row in range(0, size_y, 16):
        for lane in range(0, 256, 128):
            at = (slice(row, row + 16), slice(lane, lane + 128))
            window = [plane(j, at) for j in range(count + 2 * RADIUS)]
            for g in range(count):
                s = stiff[(base + g,) + at] * scale
                t = s * (1.0 / (FIRST_SCALE * FIRST_SCALE))
                coef[0][(base + g,) + at] = s * (1.0 / SECOND_SCALE) * window[g + RADIUS]
                coef[1][(base + g,) + at] = t * x_first(window, g)
                coef[2][(base + g,) + at] = t * ys[(g,) + at]
                coef[3][(base + g,) + at] = t * zs[(g,) + at]


def products(base, count, r, q, ya, yb, ymat, zmat, ys, zs):
    for g in range(count):
        high, low = parts(q[base + g])
        if g % 2 == 0:
            hh, hl = halo_parts(ya, yb, (base + g) // 2)
        ys[g] = dot(ymat[r["variant"] + g % 2], jnp.concatenate([high, low, hh, hl], axis=0))
        zs[g] = dot(jnp.concatenate([high, low], axis=1), zmat[...])


def elementwise(base, count, plane, r, step, q, p, out, ys, zs, coef, inject, snap, image, scale):
    size_y = r["size_y"]
    for row in range(0, size_y, 16):
        for lane in range(0, 256, 128):
            at = (slice(row, row + 16), slice(lane, lane + 128))
            below = (slice(size_y + row, size_y + row + 16), slice(lane, lane + 128))
            beside = (slice(row, row + 16), slice(256 + lane, 256 + lane + 128))
            window = [plane(j, at) for j in range(count + 2 * RADIUS)]
            for g in range(count):
                here = (base + g,) + at
                centre = window[g + RADIUS]
                first = x_first(window, g)
                second = x_second(window, g) + (ys[(g,) + at] + zs[(g,) + at])
                change = coef[0][here] * second + coef[1][here] * first
                change = change + coef[2][here] * ys[(g,) + below] + coef[3][here] * zs[(g,) + beside]
                kept = (centre + centre) - p[here]
                if step < 2:
                    kept = kept * scale
                if lane == 0:
                    added = pltpu.roll(inject[base + g, row : row + 16, :], (128 - 8 * step) % 128, 1)
                    depth = lax.broadcasted_iota(jnp.int32, (16, 128), 1)
                    kept = kept + jnp.where(depth < 8, added, 0.0)
                value = kept + change
                out[here] = value
                shown = snap[here].astype(F32) * value
                image[here] = shown if step == 0 else image[here] + shown


def mute(image, source, corner, ranges):
    size_y = image.shape[1]
    y = lax.broadcasted_iota(jnp.int32, (size_y, 128), 0) + corner[1] - source[0, 1]
    z = lax.broadcasted_iota(jnp.int32, (size_y, 128), 1) - source[0, 2]
    flat = y * y + z * z
    for dx in range(1 - MUTE, MUTE):
        at = source[0, 0] - corner[0] + dx
        inside = functools.reduce(lambda a, b: a | b, [(at >= lo) & (at < hi) for lo, hi in ranges])

        @pl.when(inside)
        def _():
            image[at, :, 0:128] = jnp.where(flat + dx * dx < MUTE * MUTE, 0.0, image[at, :, 0:128])


def split_image(image, sent, kept, core, ranges):
    (lower, _), (upper, _) = ranges

    def body(i, carry):
        sent[i] = image[jnp.where(core == 0, upper, lower) + i]
        kept[i] = image[jnp.where(core == 0, lower, upper) + i]
        return carry

    lax.fori_loop(0, sent.shape[0], body, 0)


def step_kernel(step, ranges, edges, splits, names, *refs):
    r = dict(zip(names, refs))
    q, corner = r["q"], r["corner"]
    size_x, size_y, _ = q.shape
    r["size_y"] = size_y
    r["variant"] = 2 * corner[4]
    scale = r["openness"][0, 0].astype(F32)
    coef = [r["c%d" % i] for i in range(4)]
    common = (r["ya"], r["yb"], r["ymat"], r["zmat"], r["ys"], r["zs"])
    if "snap_next" in r:
        copy = pltpu.make_async_copy(r["snaps"].at[step + 1], r["snap_next"], r["sem"])
        copy.start()

    def inflow(start, size, n):
        pairs = ((r["p_far"], r["p"]), (r["stiff_far"], r["stiff"]), (r["snaps"].at[0], r["snap"]))
        at = pl.ds(start, size)
        return [pltpu.make_async_copy(a.at[at], b.at[at], r["sems"].at[k, n]) for k, (a, b) in enumerate(pairs)]

    arriving = []
    if "sems" in r:
        low, high = ranges[0]
        groups = (high - low) // G
        for i in range(1, groups):
            arriving += inflow(low + i * G, G, i)
        arriving += inflow(high, RADIUS, groups)
        for copy_in in arriving:
            copy_in.start()

    def reader(field, base, offset):
        def plane(j, at):
            where = base - RADIUS + j
            if isinstance(where, int) and where < 0:
                return r["halo"][(0, offset + where + RADIUS) + at]
            if isinstance(where, int) and where >= size_x:
                return r["halo"][(1, offset + where - size_x) + at]
            return field[(where,) + at]

        return plane

    def prepare(base, count):
        if step == 0:
            make_coefficients(
                base, count, reader(r["buoy"], base, RADIUS), r, *common, r["stiff"], r["buoy"], coef, scale
            )

    def advance(bases, count):
        slots = [(r["ys"].at[n * count : (n + 1) * count], r["zs"].at[n * count : (n + 1) * count]) for n in range(len(bases))]
        for base, slot in zip(bases, slots):
            products(base, count, r, q, *common[:4], *slot)
        for base, slot in zip(bases, slots):
            elementwise(
                base, count, reader(q, base, 0), r, step, q, r["p"], r["out"], *slot, coef, r["inject"], r["snap"],
                r["image"], scale
            )

    for low, high in ranges:
        count = G if (high - low) % G == 0 else 4

        def body(i, carry):
            if arriving:

                @pl.when(i > 0)
                def _():
                    for copy_in in inflow(low + i * count, count, i):
                        copy_in.wait()

            prepare(low + i * count, count)
            advance([low + i * count], count)
            return carry

        lax.fori_loop(0, (high - low) // count, body, 0)
    for copy_in in arriving[-3:]:
        copy_in.wait()
    if edges:
        r["halo"][corner[3]] = r["xa"][...]
        r["halo"][1 - corner[3]] = r["xb"][...]
        prepare(0, RADIUS)
        prepare(size_x - RADIUS, RADIUS)
        advance([0, size_x - RADIUS], RADIUS)
        ranges = ranges + [(0, RADIUS), (size_x - RADIUS, size_x)]
    if step == STEPS - 1:
        mute(r["image"], r["source"], corner, ranges)
    if step == STEPS - 1:
        for n, halves in enumerate(splits):
            split_image(r["image"], r["sent%d" % n], r["kept%d" % n], corner[2], halves)
    elif edges:
        top = size_x - RADIUS
        r["sxa"][...] = r["out"][pl.ds(top * corner[3], RADIUS)]
        r["sxb"][...] = r["out"][pl.ds(top * (1 - corner[3]), RADIUS)]
        pack_strips(r["out"].at[:, 0:8], r["out"].at[:, size_y - 8 :], corner[4] == 1, r["sya"], r["syb"], 0)
    if "snap_next" in r:
        copy.wait()


def add_kernel(a, b, *rest):
    rest[-1][...] = a[...] + b[...]


def gather_kernel(splits, corner, *refs):
    out, sems = refs[-2:]
    core = corner[2]
    copies = []
    for n, ((lower, _), (upper, _)) in enumerate(splits):
        for k, (source, first, second) in enumerate(((refs[2 * n], lower, upper), (refs[2 * n + 1], upper, lower))):
            at = pl.ds(jnp.where(core == 0, first, second), source.shape[0])
            copies.append(pltpu.make_async_copy(source, out.at[at], sems.at[n, k]))
    for copy in copies:
        copy.start()
    for copy in copies:
        copy.wait()


def store_kernel(source, out, sem):
    copy = pltpu.make_async_copy(source, out, sem)
    copy.start()
    copy.wait()


VMEM = pl.BlockSpec(memory_space=pltpu.VMEM)
SMEM = pl.BlockSpec(memory_space=pltpu.SMEM)
HBM = pl.BlockSpec(memory_space=pltpu.HBM)


def placed(args, specs):
    return [a if s is SMEM else pltpu.with_memory_space_constraint(a, s.memory_space) for a, s in zip(args, specs)]


def call(kernel, name, args, specs, outs, aliases={}, scratch=(), weight=1):
    outs = [pltpu.VMEM(o, F32) if isinstance(o, tuple) else o for o in outs]
    results = pl.pallas_call(
        kernel,
        name=name,
        in_specs=specs,
        out_specs=[pl.BlockSpec(memory_space=o.memory_space) for o in outs],
        out_shape=outs,
        input_output_aliases=aliases,
        scratch_shapes=list(scratch),
        compiler_params=pltpu.CompilerParams(vmem_limit_bytes=8 << 20),
        cost_estimate=pl.CostEstimate(flops=weight, bytes_accessed=1, transcendentals=0),
    )(*placed(args, specs))
    return list(results)


def exchange(strips):
    sxa, sxb, sya, syb = strips

    def swap(strip, stride, odd):
        tiles = range(lax.axis_size("dom"))
        position = lambda i: i % 4 if stride == 1 else i // 4
        last = 3 if stride == 1 else len(tiles) // 4 - 1
        pairs = [(i, i + stride) for i in tiles if position(i) % 2 == odd and position(i) < last]
        return lax.ppermute(strip, "dom", pairs + [(b, a) for a, b in pairs])

    ya, yb = swap(sya, 1, 0), swap(syb, 1, 1)
    xa, xb = swap(sxa, 4, 1), swap(sxb, 4, 0)
    return xa, xb, ya, yb


CORES = [(i, i ^ 1) for i in range(4)]
CHIPS = [(i, i ^ 2) for i in range(4)]


def add_cores(sent, kept, after=()):
    arrived = lax.ppermute(sent, "shot", CORES)
    args = [kept, arrived] + list(after)
    return call(add_kernel, "add_cores", args, [VMEM] * len(args), [kept.shape])[0]


def add_chips(mine, after):
    arrived = lax.ppermute(mine, "shot", CHIPS)
    args, specs = [mine, arrived] + after, [VMEM] * 2 + [HBM] * len(after)
    (mine,) = call(add_kernel, "add_chips", args, specs, [mine.shape])
    return mine, lax.ppermute(mine, "shot", CORES)


def on_device(wave_prev, wave_now, stiffness, buoyancy, snapshots, traces, aperture, receivers, sources):
    index = lax.axis_index("dom")
    size_x, size_y, size_z = grid = buoyancy.shape[1:]
    corner = [index // 4 * size_x, index % 4 * size_y, lax.axis_index("shot") % 2, index // 4 % 2, index % 2]
    corner = jnp.stack(corner).astype(jnp.int32)
    places = receivers[0].T[:, None, :]
    ymat, zmat = jnp.asarray(y_matrices(size_y)), jnp.asarray(z_matrix(size_z))
    snaps = snapshots[0, :, 0]

    strips = call(
        strips_kernel, "strips", (wave_now[0, 0], buoyancy[0], corner), [HBM, HBM, SMEM],
        [(2 * RADIUS, size_y, size_z)] * 2 + [(size_x, 8, size_z)] * 2,
        scratch=[pltpu.VMEM((2, 2, size_x, 8, size_z), F32), pltpu.SemaphoreType.DMA((8,))],
    )
    halos = exchange(strips)
    fetched = [wave_now[0, 0], buoyancy[0], ymat, zmat, wave_prev[0, 0], stiffness[0], snaps]
    shapes = [a.shape for a in fetched[:-1]] + [grid]
    args = [places, traces[0], aperture, corner] + fetched
    inject, q, buoy, ymat, zmat, p, stiff, snap = call(
        fetch_kernel, "fetch", args, [VMEM, VMEM, SMEM, SMEM] + [HBM] * len(fetched),
        [(size_x, size_y, 128)] + [pltpu.VMEM(shape, a.dtype) for shape, a in zip(shapes, fetched)],
        scratch=[pltpu.VMEM((traces.shape[2], 128), BF16), pltpu.SemaphoreType.DMA((len(fetched),))],
    )

    held = dict(inject=inject, ymat=ymat, zmat=zmat, openness=aperture, source=sources, corner=corner, snaps=snaps)
    held.update(q=q, buoy=buoy, p=p, stiff=stiff, snap=snap, p_far=wave_prev[0, 0], stiff_far=stiffness[0])
    places_of = dict(openness=SMEM, source=SMEM, corner=SMEM, snaps=HBM, p_far=HBM, stiff_far=HBM)

    def run(step, ranges, edges, started, extra, splits=(), weight=1):
        ahead = not edges and step < STEPS - 1
        fresh = step == 0 and not edges
        ins = ["q", "inject", "ya", "yb", "ymat", "zmat", "openness", "source", "corner"]
        ins += (["xa", "xb"] if edges else []) + (["snaps"] if ahead else [])
        ins += ["p_far", "stiff_far"] if fresh else ["p", "snap"]
        ins += ["buoy"] if step == 0 else ["c0", "c1", "c2", "c3"]
        ins += ["stiff"] if step == 0 and edges else []
        results = ["out", "image"] + (["c0", "c1", "c2", "c3"] if step == 0 else []) + (["p", "stiff", "snap"] if fresh else [])
        given = [n for n in results if n in started]
        extra = dict(extra)
        scratch = dict(
            ys=pltpu.VMEM((G, 2 * size_y, size_z), F32), zs=pltpu.VMEM((G, size_y, 2 * size_z), F32)
        )
        if ahead:
            extra["snap_next"] = pltpu.VMEM(grid, snaps.dtype)
            scratch["sem"] = pltpu.SemaphoreType.DMA
        if fresh:
            scratch["sems"] = pltpu.SemaphoreType.DMA((3, size_x // G))
        if edges:
            scratch["halo"] = pltpu.VMEM((2,) + held["xa"].shape, F32)
        names = ins + [n + "_in" for n in given] + results + list(extra) + list(scratch)
        outs = call(
            functools.partial(step_kernel, step, ranges, edges, splits, names), "step%d" % step,
            [held[n] for n in ins + given], [places_of.get(n, VMEM) for n in ins + given],
            [pltpu.VMEM(grid, held[n].dtype if n == "snap" else F32) for n in results] + list(extra.values()),
            {len(ins) + i: results.index(n) for i, n in enumerate(given)}, scratch.values(), weight,
        )
        held.update(zip(results, outs))
        return outs[len(results) :]

    inner = [(RADIUS, size_x - RADIUS)]
    strip_x, strip_y = (RADIUS, size_y, size_z), (size_x // 2, 8, size_z)
    first = ("out", "image", "c0", "c1", "c2", "c3")
    for step in range(STEPS - 1):
        held.update(zip(("xa", "xb", "ya", "yb"), halos))
        (snap_next,) = run(step, inner, False, ("image",) if step else ("p", "stiff", "snap"), {}, weight=4 << 30)
        extra = dict(sxa=strip_x, sxb=strip_x, sya=strip_y, syb=strip_y)
        halos = exchange(run(step, [], True, first if step == 0 else ("out", "image"), extra))
        held.update(q=held["out"], p=held["q"], snap=snap_next)

    held.update(zip(("xa", "xb", "ya", "yb"), halos))
    splits, at = [], 0
    for size in (8, 10, 6):
        splits.insert(0, ((at, at + size), (size_x - at - size, size_x - at)))
        at += size

    def halves(splits):
        shapes = [(lower[1] - lower[0], size_y, size_z) for lower, _ in splits]
        return {name + str(i): shape for i, shape in enumerate(shapes) for name in ("sent", "kept")}

    early = run(STEPS - 1, inner, False, ("image",), halves(splits[:1]), splits[:1], weight=4 << 30)
    late = run(STEPS - 1, [], True, ("out", "image"), halves(splits[1:]), splits[1:], weight=4 << 30)
    sums = [add_cores(*early, after=late[:1]), add_cores(*late[:2]), add_cores(*late[2:])]
    (last,) = call(store_kernel, "store", [held["out"]], [VMEM], [pltpu.HBM(grid, F32)], {}, [pltpu.SemaphoreType.DMA])
    def gather(splits, chunks, started):
        return call(
            functools.partial(gather_kernel, splits), "gather", [corner] + chunks + started,
            [SMEM] + [VMEM] * len(chunks) + [HBM] * len(started), [pltpu.HBM(grid, F32)],
            {1 + len(chunks): 0} if started else {}, [pltpu.SemaphoreType.DMA((len(splits), 2))],
        )

    started = gather(splits[:2], [*add_chips(sums[0], []), *add_chips(sums[1], [])], [])
    (gradient,) = gather(splits[2:], [*add_chips(sums[2], started + [last])], started)
    return gradient[None], last[None, None]


def solution(mesh):
    return jax.shard_map(
        on_device,
        mesh=mesh,
        in_specs=(
            P("shot", "dom", None, None, None),
            P("shot", "dom", None, None, None),
            P("dom", None, None, None),
            P("dom", None, None, None),
            P("shot", None, "dom", None, None, None),
            P("shot", None, None),
            P("shot", "dom"),
            P("shot", None, None),
            P("shot", None),
        ),
        out_specs=(P("dom", None, None, None), P("shot", "dom", None, None, None)),
        check_vma=False,
    )
```

```python
import functools

import jax
import jax.numpy as jnp
import ml_dtypes
import numpy as np
from jax import lax
from jax.experimental import pallas as pl
from jax.experimental.pallas import tpu as pltpu
from jax.sharding import PartitionSpec as P

STEPS = 4
MUTE = 6
G = 8
RADIUS = 4

SECOND = (63.0, -7.875, 1.0, -0.0703125)
SECOND_CENTRE_Y, SECOND_CENTRE_Z = -336.0, -0.328125
SECOND_SCALE = 5040.0 / 128.0
FIRST = (21.0, -5.25, 1.0, -0.09375)
FIRST_SCALE = 840.0 / 32.0

F32 = jnp.float32
BF16 = jnp.bfloat16


def banded(size, weights, odd, centre=0.0):
    matrix = np.zeros((size, size + 2 * RADIUS), np.float32)
    for i in range(size):
        matrix[i, i + RADIUS] = centre
        for k, w in enumerate(weights, 1):
            matrix[i, i + RADIUS + k] = w
            matrix[i, i + RADIUS - k] = -w if odd else w
    return matrix


def y_matrices(size):
    both = np.concatenate([banded(size, SECOND, False, SECOND_CENTRE_Y), banded(size, FIRST, True)])
    own = both[:, RADIUS:-RADIUS]
    result = []
    for tile, parity in ((0, 0), (0, 1), (1, 0), (1, 1)):
        below, above = 8 * (1 - tile) + 4 * parity, 8 * tile + 4 * parity
        halo = np.zeros((2 * size, 16), np.float32)
        halo[:, below : below + 4] = both[:, :RADIUS]
        halo[:, above : above + 4] = both[:, -RADIUS:]
        result.append(np.concatenate([own, own, halo, halo], axis=1))
    return np.stack(result).astype(ml_dtypes.bfloat16)


def z_matrix(size):
    second = banded(size, SECOND, False, SECOND_CENTRE_Z)[:, RADIUS:-RADIUS].T
    first = banded(size, FIRST, True)[:, RADIUS:-RADIUS].T
    both = np.concatenate([second, first], axis=1)
    return np.concatenate([both, both], axis=0).astype(ml_dtypes.bfloat16)


def parts(value):
    high = value.astype(BF16)
    low = (value - high.astype(F32)).astype(BF16)
    return high, low


def dot(a, b):
    return jnp.dot(a, b, preferred_element_type=F32)


def weighted(weights, terms):
    terms = [t if w == 1.0 else w * t for w, t in zip(weights, terms)]
    return functools.reduce(lambda a, b: a + b, terms)


def x_first(window, g):
    return weighted(FIRST, [window[g + RADIUS + k] - window[g + RADIUS - k] for k in range(1, RADIUS + 1)])


def x_second(window, g):
    return weighted(SECOND, [window[g + RADIUS + k] + window[g + RADIUS - k] for k in range(1, RADIUS + 1)])


def halo_parts(first_ref, second_ref, pair):
    return parts(jnp.concatenate([first_ref[pair], second_ref[pair]], axis=0))


def pack_strips(lowest, highest, odd_tile, first_ref, second_ref, offset):
    rows = lax.broadcasted_iota(jnp.int32, lowest.shape[1:], 0)

    def body(i, carry):
        even, odd = lowest[2 * i], lowest[2 * i + 1]
        low = jnp.where(rows < 4, even, pltpu.roll(odd, 4, 0))
        even, odd = highest[2 * i], highest[2 * i + 1]
        high = jnp.where(rows < 4, pltpu.roll(even, 4, 0), odd)
        first_ref[offset + i] = jnp.where(odd_tile, low, high)
        second_ref[offset + i] = jnp.where(odd_tile, high, low)
        return carry

    lax.fori_loop(0, lowest.shape[0] // 2, body, 0, unroll=8)


def strips_kernel(q, b, corner, xa, xb, ya, yb, rows, sems):
    size_x, size_y, _ = q.shape
    top = size_x - RADIUS
    copies = []
    for i, source in enumerate((q, b)):
        at = RADIUS * i
        copies += [
            (source.at[:, 0:8], rows.at[i, 0]),
            (source.at[:, size_y - 8 : size_y], rows.at[i, 1]),
            (source.at[pl.ds(top * corner[3], RADIUS)], xa.at[at : at + RADIUS]),
            (source.at[pl.ds(top * (1 - corner[3]), RADIUS)], xb.at[at : at + RADIUS]),
        ]
    copies = [pltpu.make_async_copy(*pair, sems.at[n]) for n, pair in enumerate(copies)]
    for copy in copies:
        copy.start()
    for i in range(2):
        copies[4 * i].wait()
        copies[4 * i + 1].wait()
        pack_strips(rows.at[i, 0], rows.at[i, 1], corner[4] == 1, ya, yb, i * (size_x // 2))
    for i in range(2):
        copies[4 * i + 2].wait()
        copies[4 * i + 3].wait()


def fetch_kernel(places, amounts, openness, corner, *refs):
    count = (len(refs) - 3) // 2
    sources, targets = refs[:count], refs[count + 1 : 2 * count + 1]
    out, (weights, sems) = refs[count], refs[2 * count + 1 :]
    pairs = list(zip(sources, targets))
    whole, (previous, stiff, snaps) = pairs[:-3], pairs[-3:]
    first = slice(0, RADIUS + G)
    pairs = whole + [(a.at[first], b.at[first]) for a, b in (previous, stiff, (snaps[0].at[0], snaps[1]))]
    copies = [pltpu.make_async_copy(a, b, sems.at[n]) for n, (a, b) in enumerate(pairs)]
    for copy in copies:
        copy.start()
    size_x, size_y, lanes = out.shape
    receivers = amounts.shape[1]
    sublane = lax.broadcasted_iota(jnp.int32, (8, receivers), 0)
    at_depth = sublane == places[2]
    spread = [jnp.where(at_depth, amounts[t : t + 1], 0.0) for t in range(STEPS)]
    spread = jnp.concatenate(spread, axis=0)
    high = spread.astype(BF16).astype(F32)
    rest = spread - high
    middle = rest.astype(BF16).astype(F32)
    pieces = [high, middle, rest - middle, jnp.zeros_like(high)]
    weights[...] = jnp.concatenate(pieces, axis=0).T.astype(BF16)
    block = 8
    scale = openness[0, 0].astype(F32)
    lane = lax.broadcasted_iota(jnp.int32, (block * size_y, lanes), 1)
    local_x = places[0] - corner[0]
    rows = lax.broadcasted_iota(jnp.int32, (size_y, receivers), 0)
    at_y = jnp.where(rows == places[1] - corner[1], 1.0, 0.0).astype(BF16)

    def body(i, carry):
        hits = []
        for j in range(block):
            at_x = jnp.where(local_x == i * block + j, 1.0, 0.0).astype(BF16)
            hits.append(at_y * at_x)
        found = dot(jnp.concatenate(hits, axis=0), weights[...])
        found = found + pltpu.roll(found, lanes - 32, 1) + pltpu.roll(found, lanes - 64, 1)
        found = jnp.where(lane < 32, found * scale, 0.0)
        for j in range(block):
            out[i * block + j] = found[j * size_y : (j + 1) * size_y]
        return carry

    lax.fori_loop(0, size_x // block, body, 0)
    for copy in copies:
        copy.wait()


def make_coefficients(base, count, plane, r, ya, yb, ymat, zmat, ys, zs, stiff, buoy, coef, scale):
    size_y = r["size_y"]
    pairs = buoy.shape[0] // 2
    along_z = []
    for g in range(count):
        high, low = parts(buoy[base + g])
        if g % 2 == 0:
            hh, hl = halo_parts(ya, yb, pairs + (base + g) // 2)
        ys[g, 0:size_y] = dot(ymat[r["variant"] + g % 2, size_y:], jnp.concatenate([high, low, hh, hl], axis=0))
        along_z.append(jnp.concatenate([high, low], axis=1))
        if len(along_z) == 4:
            found = dot(jnp.concatenate(along_z, axis=0), zmat[:, 256:])
            zs[g - 3 : g + 1, :, 0:256] = found.reshape(4, size_y, 256)
            along_z = []
    for row in range(0, size_y, 16):
        for lane in range(0, 256, 128):
            at = (slice(row, row + 16), slice(lane, lane + 128))
            window = [plane(j, at) for j in range(count + 2 * RADIUS)]
            for g in range(count):
                s = stiff[(base + g,) + at] * scale
                t = s * (1.0 / (FIRST_SCALE * FIRST_SCALE))
                coef[0][(base + g,) + at] = s * (1.0 / SECOND_SCALE) * window[g + RADIUS]
                coef[1][(base + g,) + at] = t * x_first(window, g)
                coef[2][(base + g,) + at] = t * ys[(g,) + at]
                coef[3][(base + g,) + at] = t * zs[(g,) + at]


def products(base, count, r, q, ya, yb, ymat, zmat, ys, zs):
    for g in range(count):
        high, low = parts(q[base + g])
        if g % 2 == 0:
            hh, hl = halo_parts(ya, yb, (base + g) // 2)
        ys[g] = dot(ymat[r["variant"] + g % 2], jnp.concatenate([high, low, hh, hl], axis=0))
        zs[g] = dot(jnp.concatenate([high, low], axis=1), zmat[...])


def elementwise(base, count, plane, r, step, q, p, out, ys, zs, coef, inject, snap, image, scale):
    size_y = r["size_y"]
    for row in range(0, size_y, 16):
        for lane in range(0, 256, 128):
            at = (slice(row, row + 16), slice(lane, lane + 128))
            below = (slice(size_y + row, size_y + row + 16), slice(lane, lane + 128))
            beside = (slice(row, row + 16), slice(256 + lane, 256 + lane + 128))
            window = [plane(j, at) for j in range(count + 2 * RADIUS)]
            for g in range(count):
                here = (base + g,) + at
                centre = window[g + RADIUS]
                first = x_first(window, g)
                second = x_second(window, g) + (ys[(g,) + at] + zs[(g,) + at])
                change = coef[0][here] * second + coef[1][here] * first
                change = change + coef[2][here] * ys[(g,) + below] + coef[3][here] * zs[(g,) + beside]
                kept = (centre + centre) - p[here]
                if step < 2:
                    kept = kept * scale
                if lane == 0:
                    added = pltpu.roll(inject[base + g, row : row + 16, :], (128 - 8 * step) % 128, 1)
                    depth = lax.broadcasted_iota(jnp.int32, (16, 128), 1)
                    kept = kept + jnp.where(depth < 8, added, 0.0)
                value = kept + change
                out[here] = value
                shown = snap[here].astype(F32) * value
                image[here] = shown if step == 0 else image[here] + shown


def mute(image, source, corner, ranges):
    size_y = image.shape[1]
    y = lax.broadcasted_iota(jnp.int32, (size_y, 128), 0) + corner[1] - source[0, 1]
    z = lax.broadcasted_iota(jnp.int32, (size_y, 128), 1) - source[0, 2]
    flat = y * y + z * z
    for dx in range(1 - MUTE, MUTE):
        at = source[0, 0] - corner[0] + dx
        inside = functools.reduce(lambda a, b: a | b, [(at >= lo) & (at < hi) for lo, hi in ranges])

        @pl.when(inside)
        def _():
            image[at, :, 0:128] = jnp.where(flat + dx * dx < MUTE * MUTE, 0.0, image[at, :, 0:128])


def split_image(image, sent, core, ranges):
    (lower, _), (upper, _) = ranges

    def body(i, carry):
        sent[i] = image[jnp.where(core == 0, upper, lower) + i]
        return carry

    lax.fori_loop(0, sent.shape[0], body, 0)


def step_kernel(step, ranges, edges, splits, names, *refs):
    r = dict(zip(names, refs))
    q, corner = r["q"], r["corner"]
    size_x, size_y, _ = q.shape
    r["size_y"] = size_y
    r["variant"] = 2 * corner[4]
    scale = r["openness"][0, 0].astype(F32)
    coef = [r["c%d" % i] for i in range(4)]
    common = (r["ya"], r["yb"], r["ymat"], r["zmat"], r["ys"], r["zs"])
    if "snap_next" in r:
        copy = pltpu.make_async_copy(r["snaps"].at[step + 1], r["snap_next"], r["sem"])
        copy.start()

    def inflow(start, size, n):
        pairs = ((r["p_far"], r["p"]), (r["stiff_far"], r["stiff"]), (r["snaps"].at[0], r["snap"]))
        at = pl.ds(start, size)
        return [pltpu.make_async_copy(a.at[at], b.at[at], r["sems"].at[k, n]) for k, (a, b) in enumerate(pairs)]

    arriving = []
    if "sems" in r:
        low, high = ranges[0]
        groups = (high - low) // G
        for i in range(1, groups):
            arriving += inflow(low + i * G, G, i)
        arriving += inflow(high, RADIUS, groups)
        for copy_in in arriving:
            copy_in.start()

    def reader(field, base, offset):
        def plane(j, at):
            where = base - RADIUS + j
            if isinstance(where, int) and where < 0:
                return r["halo"][(0, offset + where + RADIUS) + at]
            if isinstance(where, int) and where >= size_x:
                return r["halo"][(1, offset + where - size_x) + at]
            return field[(where,) + at]

        return plane

    def prepare(base, count):
        if step == 0:
            make_coefficients(
                base, count, reader(r["buoy"], base, RADIUS), r, *common, r["stiff"], r["buoy"], coef, scale
            )

    def advance(bases, count):
        slots = [(r["ys"].at[n * count : (n + 1) * count], r["zs"].at[n * count : (n + 1) * count]) for n in range(len(bases))]
        for base, slot in zip(bases, slots):
            products(base, count, r, q, *common[:4], *slot)
        for base, slot in zip(bases, slots):
            elementwise(
                base, count, reader(q, base, 0), r, step, q, r["p"], r["out"], *slot, coef, r["inject"], r["snap"],
                r["image"], scale
            )

    for low, high in ranges:
        count = G if (high - low) % G == 0 else 4

        def body(i, carry):
            if arriving:

                @pl.when(i > 0)
                def _():
                    for copy_in in inflow(low + i * count, count, i):
                        copy_in.wait()

            prepare(low + i * count, count)
            advance([low + i * count], count)
            return carry

        lax.fori_loop(0, (high - low) // count, body, 0)
    for copy_in in arriving[-3:]:
        copy_in.wait()
    if edges:
        r["halo"][corner[3]] = r["xa"][...]
        r["halo"][1 - corner[3]] = r["xb"][...]
        prepare(0, RADIUS)
        prepare(size_x - RADIUS, RADIUS)
        advance([0, size_x - RADIUS], RADIUS)
        ranges = ranges + [(0, RADIUS), (size_x - RADIUS, size_x)]
    if step == STEPS - 1:
        mute(r["image"], r["source"], corner, ranges)
    if step == STEPS - 1:
        for n, halves in enumerate(splits):
            split_image(r["image"], r["sent%d" % n], corner[2], halves)
    elif edges:
        top = size_x - RADIUS
        r["sxa"][...] = r["out"][pl.ds(top * corner[3], RADIUS)]
        r["sxb"][...] = r["out"][pl.ds(top * (1 - corner[3]), RADIUS)]
        pack_strips(r["out"].at[:, 0:8], r["out"].at[:, size_y - 8 :], corner[4] == 1, r["sya"], r["syb"], 0)
    if "snap_next" in r:
        copy.wait()


def add_kernel(a, b, *rest):
    rest[-1][...] = a[...] + b[...]


def gather_kernel(splits, corner, *refs):
    out, sems = refs[-2:]
    core = corner[2]
    copies = []
    for n, ((lower, _), (upper, _)) in enumerate(splits):
        for k, (source, first, second) in enumerate(((refs[2 * n], lower, upper), (refs[2 * n + 1], upper, lower))):
            at = pl.ds(jnp.where(core == 0, first, second), source.shape[0])
            copies.append(pltpu.make_async_copy(source, out.at[at], sems.at[n, k]))
    for copy in copies:
        copy.start()
    for copy in copies:
        copy.wait()


def store_kernel(source, out, sem):
    copy = pltpu.make_async_copy(source, out, sem)
    copy.start()
    copy.wait()


VMEM = pl.BlockSpec(memory_space=pltpu.VMEM)
SMEM = pl.BlockSpec(memory_space=pltpu.SMEM)
HBM = pl.BlockSpec(memory_space=pltpu.HBM)


def placed(args, specs):
    return [a if s is SMEM else pltpu.with_memory_space_constraint(a, s.memory_space) for a, s in zip(args, specs)]


def call(kernel, name, args, specs, outs, aliases={}, scratch=(), weight=1):
    outs = [pltpu.VMEM(o, F32) if isinstance(o, tuple) else o for o in outs]
    results = pl.pallas_call(
        kernel,
        name=name,
        in_specs=specs,
        out_specs=[pl.BlockSpec(memory_space=o.memory_space) for o in outs],
        out_shape=outs,
        input_output_aliases=aliases,
        scratch_shapes=list(scratch),
        compiler_params=pltpu.CompilerParams(vmem_limit_bytes=8 << 20),
        cost_estimate=pl.CostEstimate(flops=weight, bytes_accessed=1, transcendentals=0),
    )(*placed(args, specs))
    return list(results)


def exchange(strips):
    sxa, sxb, sya, syb = strips

    def swap(strip, stride, odd):
        tiles = range(lax.axis_size("dom"))
        position = lambda i: i % 4 if stride == 1 else i // 4
        last = 3 if stride == 1 else len(tiles) // 4 - 1
        pairs = [(i, i + stride) for i in tiles if position(i) % 2 == odd and position(i) < last]
        return lax.ppermute(strip, "dom", pairs + [(b, a) for a, b in pairs])

    ya, yb = swap(sya, 1, 0), swap(syb, 1, 1)
    xa, xb = swap(sxa, 4, 1), swap(sxb, 4, 0)
    return xa, xb, ya, yb


CORES = [(i, i ^ 1) for i in range(4)]
CHIPS = [(i, i ^ 2) for i in range(4)]


def keep_kernel(ranges, image, arrived, corner, out):
    (lower, _), (upper, _) = ranges
    first = jnp.where(corner[2] == 0, lower, upper)

    def body(i, carry):
        out[i] = image[first + i] + arrived[i]
        return carry

    lax.fori_loop(0, out.shape[0], body, 0)


def add_cores(sent, ranges, image, corner):
    arrived = lax.ppermute(sent, "shot", CORES)
    kernel = functools.partial(keep_kernel, ranges)
    return call(kernel, "add_cores", (image, arrived, corner), [VMEM, VMEM, SMEM], [sent.shape])[0]


def add_chips(mine, after):
    arrived = lax.ppermute(mine, "shot", CHIPS)
    args, specs = [mine, arrived] + after, [VMEM] * 2 + [HBM] * len(after)
    (mine,) = call(add_kernel, "add_chips", args, specs, [mine.shape])
    return mine, lax.ppermute(mine, "shot", CORES)


def on_device(wave_prev, wave_now, stiffness, buoyancy, snapshots, traces, aperture, receivers, sources):
    index = lax.axis_index("dom")
    size_x, size_y, size_z = grid = buoyancy.shape[1:]
    corner = [index // 4 * size_x, index % 4 * size_y, lax.axis_index("shot") % 2, index // 4 % 2, index % 2]
    corner = jnp.stack(corner).astype(jnp.int32)
    places = receivers[0].T[:, None, :]
    ymat, zmat = jnp.asarray(y_matrices(size_y)), jnp.asarray(z_matrix(size_z))
    snaps = snapshots[0, :, 0]

    strips = call(
        strips_kernel, "strips", (wave_now[0, 0], buoyancy[0], corner), [HBM, HBM, SMEM],
        [(2 * RADIUS, size_y, size_z)] * 2 + [(size_x, 8, size_z)] * 2,
        scratch=[pltpu.VMEM((2, 2, size_x, 8, size_z), F32), pltpu.SemaphoreType.DMA((8,))],
    )
    halos = exchange(strips)
    fetched = [wave_now[0, 0], buoyancy[0], ymat, zmat, wave_prev[0, 0], stiffness[0], snaps]
    shapes = [a.shape for a in fetched[:-1]] + [grid]
    args = [places, traces[0], aperture, corner] + fetched
    inject, q, buoy, ymat, zmat, p, stiff, snap = call(
        fetch_kernel, "fetch", args, [VMEM, VMEM, SMEM, SMEM] + [HBM] * len(fetched),
        [(size_x, size_y, 128)] + [pltpu.VMEM(shape, a.dtype) for shape, a in zip(shapes, fetched)],
        scratch=[pltpu.VMEM((traces.shape[2], 128), BF16), pltpu.SemaphoreType.DMA((len(fetched),))],
    )

    held = dict(inject=inject, ymat=ymat, zmat=zmat, openness=aperture, source=sources, corner=corner, snaps=snaps)
    held.update(q=q, buoy=buoy, p=p, stiff=stiff, snap=snap, p_far=wave_prev[0, 0], stiff_far=stiffness[0])
    places_of = dict(openness=SMEM, source=SMEM, corner=SMEM, snaps=HBM, p_far=HBM, stiff_far=HBM)

    def run(step, ranges, edges, started, extra, splits=(), weight=1):
        ahead = not edges and step < STEPS - 1
        fresh = step == 0 and not edges
        ins = ["q", "inject", "ya", "yb", "ymat", "zmat", "openness", "source", "corner"]
        ins += (["xa", "xb"] if edges else []) + (["snaps"] if ahead else [])
        ins += ["p_far", "stiff_far"] if fresh else ["p", "snap"]
        ins += ["buoy"] if step == 0 else ["c0", "c1", "c2", "c3"]
        ins += ["stiff"] if step == 0 and edges else []
        results = ["out", "image"] + (["c0", "c1", "c2", "c3"] if step == 0 else []) + (["p", "stiff", "snap"] if fresh else [])
        given = [n for n in results if n in started]
        extra = dict(extra)
        scratch = dict(
            ys=pltpu.VMEM((G, 2 * size_y, size_z), F32), zs=pltpu.VMEM((G, size_y, 2 * size_z), F32)
        )
        if ahead:
            extra["snap_next"] = pltpu.VMEM(grid, snaps.dtype)
            scratch["sem"] = pltpu.SemaphoreType.DMA
        if fresh:
            scratch["sems"] = pltpu.SemaphoreType.DMA((3, size_x // G))
        if edges:
            scratch["halo"] = pltpu.VMEM((2,) + held["xa"].shape, F32)
        names = ins + [n + "_in" for n in given] + results + list(extra) + list(scratch)
        outs = call(
            functools.partial(step_kernel, step, ranges, edges, splits, names), "step%d" % step,
            [held[n] for n in ins + given], [places_of.get(n, VMEM) for n in ins + given],
            [pltpu.VMEM(grid, held[n].dtype if n == "snap" else F32) for n in results] + list(extra.values()),
            {len(ins) + i: results.index(n) for i, n in enumerate(given)}, scratch.values(), weight,
        )
        held.update(zip(results, outs))
        return outs[len(results) :]

    inner = [(RADIUS, size_x - RADIUS)]
    strip_x, strip_y = (RADIUS, size_y, size_z), (size_x // 2, 8, size_z)
    first = ("out", "image", "c0", "c1", "c2", "c3")
    for step in range(STEPS - 1):
        held.update(zip(("xa", "xb", "ya", "yb"), halos))
        (snap_next,) = run(step, inner, False, ("image",) if step else ("p", "stiff", "snap"), {}, weight=4 << 30)
        extra = dict(sxa=strip_x, sxb=strip_x, sya=strip_y, syb=strip_y)
        halos = exchange(run(step, [], True, first if step == 0 else ("out", "image"), extra))
        held.update(q=held["out"], p=held["q"], snap=snap_next)

    held.update(zip(("xa", "xb", "ya", "yb"), halos))
    splits, at = [], 0
    for size in (8, 10, 6):
        splits.insert(0, ((at, at + size), (size_x - at - size, size_x - at)))
        at += size

    def halves(splits):
        shapes = [(lower[1] - lower[0], size_y, size_z) for lower, _ in splits]
        return {name + str(i): shape for i, shape in enumerate(shapes) for name in ("sent",)}

    early = run(STEPS - 1, inner, False, ("image",), halves(splits[:1]), splits[:1], weight=4 << 30)
    late = run(STEPS - 1, [], True, ("out", "image"), halves(splits[1:]), splits[1:], weight=4 << 30)
    sums = [add_cores(sent, ranges, held["image"], corner) for sent, ranges in zip(early + late, splits)]
    (last,) = call(store_kernel, "store", [held["out"]], [VMEM], [pltpu.HBM(grid, F32)], {}, [pltpu.SemaphoreType.DMA])
    def gather(splits, chunks, started):
        return call(
            functools.partial(gather_kernel, splits), "gather", [corner] + chunks + started,
            [SMEM] + [VMEM] * len(chunks) + [HBM] * len(started), [pltpu.HBM(grid, F32)],
            {1 + len(chunks): 0} if started else {}, [pltpu.SemaphoreType.DMA((len(splits), 2))],
        )

    started = gather(splits[:2], [*add_chips(sums[0], []), *add_chips(sums[1], [])], [])
    (gradient,) = gather(splits[2:], [*add_chips(sums[2], started + [last])], started)
    return gradient[None], last[None, None]


def solution(mesh):
    return jax.shard_map(
        on_device,
        mesh=mesh,
        in_specs=(
            P("shot", "dom", None, None, None),
            P("shot", "dom", None, None, None),
            P("dom", None, None, None),
            P("dom", None, None, None),
            P("shot", None, "dom", None, None, None),
            P("shot", None, None),
            P("shot", "dom"),
            P("shot", None, None),
            P("shot", None),
        ),
        out_specs=(P("dom", None, None, None), P("shot", "dom", None, None, None)),
        check_vma=False,
    )
```
